32 devices in a mesh: dp: 16 (over z, y, core), tensor: 2 (over x).
Axes of the slice: x: 2, y: 2, z: 4, core: 2. Of those that a mesh axis runs over, the one named last changes fastest.
Arguments:
- tokens: bfloat16 [32768, 1024], P(('dp', 'tensor')), may hold values from -6 to 6
- lengths: int32 [16, 16], P('dp'), may hold values from 1 to 1024, 2048 in all within a row
- routes: int32 [32768, 8], P('dp'), may hold values from 0 to 31, all different within a row; in each aligned block of 2048 rows (0 to 2047, 2048 to 4095, ...) at most 768 rows name the same one
- norm1_gain: bfloat16 [1024], P('dp'), may hold values from 0.5 to 1.5
- w_query: bfloat16 [1024, 1024], P('dp', 'tensor'), may hold values from -0.1875 to 0.1875
- key_projection: bfloat16 [1024, 512], P('dp', 'tensor'), may hold values from -0.1875 to 0.1875
- value_projection: bfloat16 [1024, 512], P('dp', 'tensor'), may hold values from -0.1875 to 0.1875
- w_out: bfloat16 [1024, 1024], P('tensor', 'dp'), may hold values from -0.75 to 0.75
- norm2_gain: bfloat16 [1024], P('dp'), may hold values from 0.5 to 1.5
- w_router: bfloat16 [1024, 32], P('dp'), may hold values from -0.09375 to 0.09375
- w_gate: bfloat16 [32, 1024, 512], P('tensor', 'dp'), may hold values from -0.1875 to 0.1875
- w_up: bfloat16 [32, 1024, 512], P('tensor', 'dp'), may hold values from -0.1875 to 0.1875
- w_down: bfloat16 [32, 512, 1024], P('tensor', 'dp'), may hold values from -1 to 1
- cotangent: bfloat16 [32768, 1024], P(('dp', 'tensor')), may hold values from -6 to 6
Outputs:
- output: bfloat16 [32768, 1024], P(('dp', 'tensor'))
- grad_tokens: bfloat16 [32768, 1024], P(('dp', 'tensor'))
- grad_norm1: float32 [1024], P('dp')
- grad_query: float32 [1024, 1024], P('dp', 'tensor')
- grad_key: float32 [1024, 512], P('dp', 'tensor')
- grad_value: float32 [1024, 512], P('dp', 'tensor')
- grad_out: float32 [1024, 1024], P('tensor', 'dp')
- grad_norm2: float32 [1024], P('dp')
- grad_router: float32 [1024, 32], P('dp')
- grad_gate: float32 [32, 1024, 512], P('tensor', 'dp')
- grad_up: float32 [32, 1024, 512], P('tensor', 'dp')
- grad_down: float32 [32, 512, 1024], P('tensor', 'dp')
The draws below stay inside these ranges and needn't reach their ends.
Inputs may be any that keep to these rules, and one draw needn't show every extreme that they name: `routes`: in each group of 2048 rows no expert is named by more than 768 rows, a bound that some block reaches; a row names 8 different experts. `lengths`: each row sums to 2048; its largest entry is exactly 1024.
All inputs are finite; a program needn't handle non-finite values.
Results may differ from the reference program's by a relative error of at most 0.023.
Values may be sent and summed in bfloat16 or wider, within the bound.
No kernel may reach another device: no remote copies, remote signals or barrier semaphores. Data moves between devices by JAX's collectives and lax.ppermute only.
A program may use at most 448 MiB of HBM per device.

```python
import math
import jax
import jax.numpy as jnp
import numpy as np
from jax import lax

MODEL_WIDTH = 1024
QUERY_HEADS = 16
KEY_VALUE_HEADS = 8
HEAD_SIZE = 64
EXPERTS = 32
FF_E = 512
TOP = 8
GRP = 2048
SEQS = 16
MAXLEN = 1024
QUERY_BLOCK_ROWS = 512
KW = 1536
CAP = 768
GROUPS = 16
TOKENS = 32768


def levels(key, shape, pieces, smallest, largest):
    def one(axis_at, parts):
        steps = jax.random.uniform(jax.random.fold_in(jax.random.fold_in(key, 6), axis_at), (parts,), jnp.float32, smallest / len(pieces), largest / len(pieces))
        return jnp.repeat(jnp.exp(steps), shape[axis_at] // parts).reshape((-1,) + (1,) * (len(shape) - axis_at - 1))

    loudness = one(*pieces[0])
    for cut in pieces[1:]:
        loudness = loudness * one(*cut)
    return loudness


def length_profile(amount, total, most, skew):
    loads = [(1 << 20) // math.isqrt(rank ** skew) + 1 for rank in range(2, amount + 1)]
    rest, holding = total - most - (amount - 1), [1] * (amount - 1)
    while rest > 0:
        free = [i for i in range(amount - 1) if holding[i] < most]
        pool, left = sum([loads[i] for i in free]), rest
        for i in free:
            extra = min(most - holding[i], max(1, left * loads[i] // pool), rest)
            holding[i] = holding[i] + extra
            rest = rest - extra
    return np.array([most] + holding)


def uneven_parts(stream_key, amount, total, reach, skew):
    if amount == 2:
        one = jax.random.randint(stream_key, (), max(1, total - reach), min(reach, total - 1) + 1)
        return jnp.stack([one, total - one])
    sizes = jnp.asarray(length_profile(amount, total, reach, skew), jnp.int32)
    pairs = (amount - 1) // 2
    donor, sink = sizes[1:1 + 2 * pairs:2], sizes[2:2 + 2 * pairs:2]
    margin = jnp.minimum(donor - 1, reach - sink)
    moved = jax.random.randint(jax.random.fold_in(stream_key, 1), (pairs,), 0, 1 << 20) % (margin + 1)
    sizes = sizes.at[1:1 + 2 * pairs:2].set(donor - moved).at[2:2 + 2 * pairs:2].set(sink + moved)
    return sizes[jax.random.permutation(jax.random.fold_in(stream_key, 2), amount)]


def assign_block(stream_key, own, number, rows, number_of, top, limit, slope):
    ranking = jax.random.permutation(stream_key, number_of)
    packed, common = shares(number_of, rows * top, limit, slope, True), shares(number_of, rows * top, limit, slope, False)
    places = jnp.arange(number_of)

    def named(sizes, turn):
        used = int((sizes > 0).sum())
        fixed = max(1, used // 4)
        moved = fixed + (places - fixed + turn * (used - fixed)) % max(1, number_of - fixed)
        return jnp.zeros((number_of,), jnp.int32).at[ranking[jnp.where(places < fixed, places, moved)]].set(jnp.asarray(sizes, jnp.int32))

    sizes = jnp.where(number % 4 == 0, named(packed, number // 4), named(common, number - number // 4 - 1))
    mixed = jax.random.permutation(jax.random.fold_in(own, 3), number_of)
    giver, taker = mixed[0:number_of // 2 * 2:2], mixed[1:number_of // 2 * 2:2]
    slack = jnp.minimum(sizes[giver] - 1, limit - sizes[taker]) // 2
    slack = jnp.where((giver == ranking[0]) | (taker == ranking[0]) | (sizes[taker] == 0), 0, jnp.maximum(slack, 0))
    moved = jax.random.randint(jax.random.fold_in(own, 4), (number_of // 2,), 0, 1 << 20) % (slack + 1)
    sizes = sizes.at[giver].add(-moved).at[taker].add(moved)
    labels = jnp.searchsorted(jnp.cumsum(sizes), jnp.arange(rows * top), side="right").astype(jnp.int32)
    table = labels.reshape(top, rows).T
    table = table[jax.random.permutation(jax.random.fold_in(own, 1), rows)]
    turn = jax.random.randint(jax.random.fold_in(own, 2), (rows, 1), 0, top)
    return jnp.take_along_axis(table, (jnp.arange(top)[None, :] + turn) % top, axis=1)


def shares(number_of, total, most, lean, full):
    loads = [(1 << 20) // math.isqrt(standing ** lean) + 1 for standing in range(1, number_of + 1)]
    largest = most if full else min(most, max(-(-total // number_of), total * loads[0] // sum(loads)))
    least = 1 if total - largest >= number_of - 1 else 0
    holding, rest = [largest] + [least] * (number_of - 1), total - largest - least * (number_of - 1)
    while rest > 0:
        free = [i for i in range(1, number_of) if holding[i] < largest] or [i for i in range(1, number_of) if holding[i] < most]
        pool, budget = sum([loads[i] for i in free]), rest
        for i in free:
            extra = min(most - holding[i], max(1, budget * loads[i] // pool), rest)
            holding[i] = holding[i] + extra
            rest = rest - extra
    return np.array(holding)


def centred(rng, dims, width, most, pieces=(), kind=jnp.bfloat16):
    loudness = levels(rng, dims, pieces, -0.22, 0.18) if pieces else 1.0
    array = jax.random.normal(rng, dims, jnp.float32) * width * loudness
    return jnp.minimum(jnp.maximum(array, -most), most).astype(kind)


def setup_inputs(seed: int = 0) -> dict:
    key_list = jax.random.split(jax.random.key(seed), 15)
    tokens = centred(key_list[0], (TOKENS, MODEL_WIDTH), 1.0, 6.0, ((0, 32),))
    lengths = jax.vmap(lambda own: uneven_parts(own, SEQS, GRP, MAXLEN, 2))(jax.random.split(key_list[1], GROUPS)).reshape((GROUPS, SEQS)).astype(jnp.int32)
    routes_keys = jax.random.split(jax.random.fold_in(key_list[2], 1), TOKENS // GRP)
    routes_turns = jax.random.permutation(jax.random.fold_in(key_list[2], 3), TOKENS // GRP)
    routes = jax.vmap(lambda own, number: assign_block(jax.random.fold_in(key_list[2], 2), own, number, GRP, EXPERTS, TOP, CAP, 1))(routes_keys, routes_turns).reshape((TOKENS, TOP))
    norm1_gain = jnp.clip(1.0 + 0.1 * jax.random.normal(key_list[3], (MODEL_WIDTH,), jnp.float32), 0.5, 1.5).astype(jnp.bfloat16)
    w_query = centred(key_list[4], (MODEL_WIDTH, QUERY_HEADS * HEAD_SIZE), MODEL_WIDTH ** -0.5, 0.1875, ((0, 16), (1, 2)))
    key_projection = centred(key_list[5], (MODEL_WIDTH, KEY_VALUE_HEADS * HEAD_SIZE), MODEL_WIDTH ** -0.5, 0.1875, ((0, 16), (1, 2)))
    value_projection = centred(key_list[6], (MODEL_WIDTH, KEY_VALUE_HEADS * HEAD_SIZE), MODEL_WIDTH ** -0.5, 0.1875, ((0, 16), (1, 2)))
    w_out = centred(key_list[7], (QUERY_HEADS * HEAD_SIZE, MODEL_WIDTH), (QUERY_HEADS * HEAD_SIZE // 16) ** -0.5, 0.75, ((0, 2), (1, 16)))
    norm2_gain = jnp.clip(1.0 + 0.1 * jax.random.normal(key_list[8], (MODEL_WIDTH,), jnp.float32), 0.5, 1.5).astype(jnp.bfloat16)
    w_router = centred(key_list[9], (MODEL_WIDTH, EXPERTS), (4 * MODEL_WIDTH) ** -0.5, 0.09375, ((0, 16),))
    w_gate = centred(key_list[10], (EXPERTS, MODEL_WIDTH, FF_E), MODEL_WIDTH ** -0.5, 0.1875, ((0, 2), (1, 16)))
    w_up = centred(key_list[11], (EXPERTS, MODEL_WIDTH, FF_E), MODEL_WIDTH ** -0.5, 0.1875, ((0, 2), (1, 16)))
    w_down = centred(key_list[12], (EXPERTS, FF_E, MODEL_WIDTH), (FF_E // 16) ** -0.5, 1.0, ((0, 2), (1, 16)))
    cotangent = centred(key_list[13], (TOKENS, MODEL_WIDTH), 1.0, 6.0, ((0, 32),))
    return dict(tokens=tokens, lengths=lengths, routes=routes, norm1_gain=norm1_gain, w_query=w_query, key_projection=key_projection, value_projection=value_projection, w_out=w_out, norm2_gain=norm2_gain, w_router=w_router, w_gate=w_gate, w_up=w_up, w_down=w_down, cotangent=cotangent)


@jax.custom_vjp
def reduced_precision(v):
    return lax.optimization_barrier(v.astype(jnp.bfloat16)).astype(jnp.float32)

@jax.custom_vjp
def reduced_backward(v):
    return v

def low_keep(v):
    return (reduced_precision(v), None)

def low_pass(kept, grad):
    return (grad,)

def back_keep(v):
    return (v, None)

def back_low(kept, grad):
    return (reduced_precision(grad),)
reduced_precision.defvjp(low_keep, low_pass)
reduced_backward.defvjp(back_keep, back_low)
exact_mode = lax.Precision.HIGHEST

def precise_product(left, right):
    return jnp.dot(left, right, precision=exact_mode)

def rms_norm(values, gain):
    inverse = lax.rsqrt(lax.optimization_barrier(jnp.mean(values * values, axis=-1, keepdims=True)) + 1e-06)
    return values * inverse * gain

def seq_layout(seq_lengths, overall_rows):
    ends = jnp.cumsum(seq_lengths).astype(jnp.int32)
    row_index = jnp.arange(overall_rows, dtype=jnp.int32)
    segment = lax.optimization_barrier(jnp.sum((row_index[:, None] >= ends[None, :]).astype(jnp.int32), axis=1)).astype(jnp.int32)
    starts = (ends - seq_lengths).astype(jnp.int32)
    which = segment[:, None] == jnp.arange(seq_lengths.shape[0], dtype=jnp.int32)[None, :]
    first_row = lax.optimization_barrier(jnp.sum(jnp.where(which, starts[None, :], 0), axis=1)).astype(jnp.int32)
    return (segment, row_index - first_row)

def rope_tables(position):
    half_width = HEAD_SIZE // 2
    frequency = 10000.0 ** (-2.0 * jnp.arange(half_width, dtype=jnp.float32) / HEAD_SIZE)
    angles = position.astype(jnp.float32)[:, None] * frequency[None, :]
    return (jnp.cos(angles)[:, None, :], jnp.sin(angles)[:, None, :])

def apply_rotary(values, cosine_table, sine_table):
    half_width = values.shape[-1] // 2
    first_half = values[..., :half_width]
    second_half = values[..., half_width:]
    return jnp.concatenate([first_half * cosine_table - second_half * sine_table, second_half * cosine_table + first_half * sine_table], axis=-1)

def attend(query_matrix, rotated_keys, value_vectors, segment):
    overall_rows = query_matrix.shape[0]

    def one_block(block_id):
        query_first_row = block_id * QUERY_BLOCK_ROWS
        key_start = jnp.clip(query_first_row - MAXLEN, 0, overall_rows - KW).astype(jnp.int32)
        query_tile = lax.dynamic_slice_in_dim(query_matrix, query_first_row, QUERY_BLOCK_ROWS, 0).reshape(QUERY_BLOCK_ROWS, KEY_VALUE_HEADS, QUERY_HEADS // KEY_VALUE_HEADS, HEAD_SIZE)
        key_block = lax.dynamic_slice_in_dim(rotated_keys, key_start, KW, 0)
        value_block = lax.dynamic_slice_in_dim(value_vectors, key_start, KW, 0)
        query_seg = lax.dynamic_slice_in_dim(segment, query_first_row, QUERY_BLOCK_ROWS, 0)
        key_seg = lax.dynamic_slice_in_dim(segment, key_start, KW, 0)
        query_index = query_first_row + jnp.arange(QUERY_BLOCK_ROWS, dtype=jnp.int32)
        key_index = key_start + jnp.arange(KW, dtype=jnp.int32)
        allowed = (query_seg[:, None] == key_seg[None, :]) & (key_index[None, :] <= query_index[:, None])
        scores = reduced_backward(jnp.einsum('qhgd,khd->hgqk', query_tile, key_block, precision=exact_mode) * HEAD_SIZE ** (-0.5))
        scores = jnp.where(allowed, scores, -1000000000.0)
        probs = reduced_precision(jax.nn.softmax(scores, axis=-1))
        mixed = jnp.einsum('hgqk,khd->qhgd', probs, value_block, precision=exact_mode)
        return mixed.reshape(QUERY_BLOCK_ROWS, QUERY_HEADS * HEAD_SIZE)
    blocks = lax.map(jax.checkpoint(one_block), jnp.arange(overall_rows // QUERY_BLOCK_ROWS, dtype=jnp.int32))
    return blocks.reshape(overall_rows, QUERY_HEADS * HEAD_SIZE)

def experts(hidden_two, gates, routes, w_gate, w_up, w_down):
    overall_rows = hidden_two.shape[0]
    names = jnp.arange(EXPERTS, dtype=jnp.int32)
    match = routes[:, :, None] == names[None, None, :]
    member = jnp.any(match, axis=1)
    share = lax.optimization_barrier(jnp.sum(jnp.where(match, gates[:, :, None], 0.0), axis=1))
    slot = jnp.cumsum(member.astype(jnp.int32), axis=0).astype(jnp.int32) - 1
    slot = jnp.where(member, slot, CAP)
    row_index = jnp.broadcast_to(jnp.arange(overall_rows, dtype=jnp.int32)[:, None], (overall_rows, EXPERTS))
    expert_index = jnp.broadcast_to(names[None, :], (overall_rows, EXPERTS))
    table = jnp.zeros((EXPERTS, CAP), jnp.int32).at[expert_index, slot].set(row_index, mode='drop')
    filled = lax.optimization_barrier(jnp.sum(member.astype(jnp.int32), axis=0)).astype(jnp.int32)
    valid = jnp.arange(CAP, dtype=jnp.int32)[None, :] < filled[:, None]
    slot_gate = jnp.where(valid, jnp.take_along_axis(share.T, table, axis=1), 0.0)
    picked = hidden_two[table]
    gate_lin = reduced_backward(jnp.einsum('ecd,edf->ecf', picked, w_gate, precision=exact_mode))
    up_lin = reduced_backward(jnp.einsum('ecd,edf->ecf', picked, w_up, precision=exact_mode))
    hidden = reduced_precision(jax.nn.silu(gate_lin) * up_lin)
    expert_out = reduced_backward(jnp.einsum('ecf,efd->ecd', hidden, w_down, precision=exact_mode))
    weighted = (slot_gate[:, :, None] * expert_out).reshape(-1, hidden_two.shape[1])
    return jnp.zeros_like(hidden_two).at[table.reshape(-1)].add(weighted)

def forward(params, inputs, routes, segment, position):
    gain_one, query_weight, key_matrix, value_matrix, out_weight, gain_two, router_weight, w_gate, w_up, w_down = params
    overall_rows = inputs.shape[0]
    cosine_table, sine_table = rope_tables(position)
    first_hidden = reduced_precision(rms_norm(inputs, gain_one))
    query_matrix = reduced_precision(apply_rotary(reduced_backward(precise_product(first_hidden, query_weight)).reshape(overall_rows, QUERY_HEADS, HEAD_SIZE), cosine_table, sine_table))
    rotated_keys = reduced_precision(apply_rotary(reduced_backward(precise_product(first_hidden, key_matrix)).reshape(overall_rows, KEY_VALUE_HEADS, HEAD_SIZE), cosine_table, sine_table))
    value_vectors = reduced_precision(reduced_backward(precise_product(first_hidden, value_matrix))).reshape(overall_rows, KEY_VALUE_HEADS, HEAD_SIZE)
    attended = reduced_precision(reduced_backward(attend(query_matrix, rotated_keys, value_vectors, segment)))
    residual_two = inputs + reduced_backward(precise_product(attended, out_weight))
    hidden_two = reduced_precision(rms_norm(residual_two, gain_two))
    logits = precise_product(hidden_two, router_weight)
    gates = reduced_precision(jax.nn.softmax(jnp.take_along_axis(logits, routes, axis=1), axis=-1))
    return residual_two + experts(hidden_two, gates, routes, w_gate, w_up, w_down)

def reference(tokens, lengths, routes, norm1_gain, w_query, key_projection, value_projection, w_out, norm2_gain, w_router, w_gate, w_up, w_down, cotangent):
    params = tuple((p.astype(jnp.float32) for p in (norm1_gain, w_query, key_projection, value_projection, w_out, norm2_gain, w_router, w_gate, w_up, w_down)))
    groups = lengths.shape[0]
    inputs_all = tokens.astype(jnp.float32).reshape(groups, GRP, MODEL_WIDTH)
    cot_all = cotangent.astype(jnp.float32).reshape(groups, GRP, MODEL_WIDTH)
    routes_all = routes.reshape(groups, GRP, TOP)
    zeros_all = tuple((jnp.zeros_like(p) for p in params))

    def step(totals, item):
        inputs, cot_rows, group_routes, group_lengths = item
        segment, position = seq_layout(group_lengths, GRP)

        def run(weights, rows_in):
            return forward(weights, rows_in, group_routes, segment, position)
        result, pull = jax.vjp(run, params, inputs)
        grad_params, grad_rows = pull(cot_rows)
        totals = tuple((t + g for t, g in zip(totals, grad_params)))
        return (totals, (result.astype(jnp.bfloat16), grad_rows.astype(jnp.bfloat16)))
    totals, (results, grad_rows) = lax.scan(step, zeros_all, (inputs_all, cot_all, routes_all, lengths))
    output = results.reshape(groups * GRP, MODEL_WIDTH)
    grad_tokens = grad_rows.reshape(groups * GRP, MODEL_WIDTH)
    return (output, grad_tokens, totals[0], totals[1], totals[2], totals[3], totals[4], totals[5], totals[6], totals[7], totals[8], totals[9])
```

```python
import functools

import jax
import jax.numpy as jnp
from jax import lax
from jax.experimental import pallas as pl
from jax.experimental.pallas import tpu as pltpu
from jax.sharding import PartitionSpec as P

QUERY_HEADS = 16
KEY_VALUE_HEADS = 8
HEAD_SIZE = 64
HALF = HEAD_SIZE // 2
EXPERTS = 32
CAP = 768
TILE = 256
BLOCK = 256
STEP = 16
EXPERT_CALLS = 4
KERNEL_COST = pl.CostEstimate(flops=1, bytes_accessed=150 * 10**6, transcendentals=0)

exact_mode = lax.Precision.HIGHEST
F32 = jnp.float32
BF16 = jnp.bfloat16
NEG = -1e30


def dot(a, b, ca, cb):
    return lax.dot_general(a, b, (((ca,), (cb,)), ((), ())), preferred_element_type=F32)


def z_core_shape(dp):
    return (4, 2, 2) if dp == 16 else None


def gather_rows(x, axis="tensor"):
    n = lax.axis_size(axis)
    if n != 2:
        return lax.all_gather(x, axis, axis=0, tiled=True)
    rank = lax.axis_index(axis)
    other = lax.ppermute(x, axis, [(0, 1), (1, 0)])
    first = rank == 0
    return jnp.concatenate([jnp.where(first, x, other), jnp.where(first, other, x)], axis=0)


def scatter_rows(x, axis="tensor"):
    n = lax.axis_size(axis)
    rows = x.shape[0] // n
    if n != 2:
        return lax.psum_scatter(x, axis, scatter_dimension=0, tiled=True).astype(F32)
    rank = lax.axis_index(axis)
    sent = lax.ppermute(
        lax.dynamic_slice_in_dim(x, (1 - rank) * rows, rows, 0), axis, [(0, 1), (1, 0)]
    )
    own = lax.dynamic_slice_in_dim(x, rank * rows, rows, 0)
    return own.astype(F32) + sent.astype(F32)


def dp_pairs(move):
    pairs = []
    for z in range(4):
        for y in range(2):
            for c in range(2):
                tz, ty, tc = move(z, y, c)
                pairs.append((z * 4 + y * 2 + c, tz * 4 + ty * 2 + tc))
    return pairs


CORE_PAIRS = dp_pairs(lambda z, y, c: (z, y, 1 - c))
Y_PAIRS = dp_pairs(lambda z, y, c: (z, 1 - y, c))
Z_PAIRS = {k: dp_pairs(lambda z, y, c, k=k: ((z + k) % 4, y, c)) for k in (1, 2, 3)}


def place(own, index, parts):
    buf = jnp.zeros((len(parts) + 1,) + own.shape, own.dtype)
    for i, a in [(index, own)] + parts:
        buf = lax.dynamic_update_index_in_dim(buf, a, i, 0)
    return buf


def gather_dp(x):
    n = lax.axis_size("dp")
    if z_core_shape(n) is None:
        return lax.all_gather(x, "dp", axis=0, tiled=False)
    me = lax.axis_index("dp")
    z, y, c = me // 4, (me // 2) % 2, me % 2
    parts = [((z - k) % 4, lax.ppermute(x, "dp", Z_PAIRS[k])) for k in (1, 3, 2)]
    buf = place(x, z, parts)
    buf = place(buf, y, [(1 - y, lax.ppermute(buf, "dp", Y_PAIRS))])
    buf = place(buf, c, [(1 - c, lax.ppermute(buf, "dp", CORE_PAIRS))])
    return jnp.transpose(buf, (2, 1, 0) + tuple(range(3, buf.ndim))).reshape((n,) + x.shape)


def at(a, i, axis):
    return lax.dynamic_index_in_dim(a, i, axis, keepdims=False)


def line_place():
    me = lax.axis_index("dp")
    return me // 4, (me // 2) % 2


class Reduce:
    def __init__(self, keep, send):
        self.by_hand = z_core_shape(lax.axis_size("dp")) is not None
        self.keep, self.send = keep, send
        self.stage = 0

    def sends(self):
        if not self.by_hand:
            return []
        if self.stage == 0:
            return [self.send]
        z, y = line_place()
        if self.stage == 1:
            self.keep = self.keep.reshape((4, 2) + self.keep.shape[1:])
            self.core = self.core.reshape(self.keep.shape)
            return [
                (
                    at(self.keep, 1 - y, 1).astype(F32) + at(self.core, 1 - y, 1).astype(F32)
                ).astype(BF16)
            ]

        def line(i):
            return (
                at(at(self.keep, y, 1), i, 0).astype(F32)
                + at(at(self.core, y, 1), i, 0).astype(F32)
                + at(self.over, i, 0).astype(F32)
            )

        self.own = line(z)
        return [line((z + k) % 4).astype(BF16) for k in (2, 1, 3)]

    def move(self, sent):
        if not self.by_hand:
            return []
        pairs = ([CORE_PAIRS], [Y_PAIRS], [Z_PAIRS[k] for k in (2, 1, 3)])[self.stage]
        return [lax.ppermute(a, "dp", p) for a, p in zip(sent, pairs)]

    def take(self, got):
        if self.by_hand:
            if self.stage == 0:
                (self.core,) = got
            elif self.stage == 1:
                (self.over,) = got
            else:
                self.parts = got
        self.stage += 1

    def result(self):
        n = lax.axis_size("dp")
        if not self.by_hand:
            even = lax.axis_index("dp") % 2 == 0
            first = jnp.where(even, self.keep, self.send)
            second = jnp.where(even, self.send, self.keep)
            both = jnp.stack([first, second], axis=1).reshape((n,) + self.keep.shape[1:])
            return lax.psum_scatter(both, "dp", scatter_dimension=0, tiled=False).astype(F32)
        total = self.own
        for a in self.parts:
            total = total + a.astype(F32)
        return total


def phase(work, inputs, reduces):
    sends = [r.sends() for r in reduces]
    (inputs, sends) = lax.optimization_barrier((list(inputs), sends))
    results = work(*inputs)
    moved = [r.move(sent) for r, sent in zip(reduces, sends)]
    results, moved = lax.optimization_barrier((results, moved))
    for r, got in zip(reduces, moved):
        r.take(got)
    return results


def rms_norm(values, gain):
    inverse = lax.rsqrt(jnp.mean(values * values, axis=-1, keepdims=True) + 1e-06)
    return (values * inverse * gain, inverse)


def rms_back(grad_rows, values, inverse, gain):
    scaled = grad_rows * gain
    gain_grad = jnp.sum(grad_rows * values * inverse, axis=0)
    inner = jnp.mean(scaled * values, axis=-1, keepdims=True)
    return (inverse * scaled - values * inverse * inverse * inverse * inner, gain_grad)


def rope_t(values, cosine, sine):
    rows = values.shape[1]
    v = values.reshape(-1, 2, HALF, rows)
    one, two = v[:, 0], v[:, 1]
    return jnp.stack(
        [one * cosine - two * sine, two * cosine + one * sine], axis=1
    ).reshape(values.shape)


def mask_of(start, j, i, bq):
    key = j * BLOCK + lax.broadcasted_iota(jnp.int32, (BLOCK, 2 * bq), 0)
    query = lax.broadcasted_iota(jnp.int32, (BLOCK, 2 * bq), 1)
    query = i * bq + jnp.where(query >= bq, query - bq, query)
    return (key >= start) & (key <= query)


def attend_kernel(low, q_ref, k_ref, v_ref, start_ref, o_ref, lse_ref):
    i = pl.program_id(1)
    bq = BLOCK
    q = q_ref[...]
    qs = jnp.concatenate([q[:HEAD_SIZE], q[HEAD_SIZE:]], axis=1)
    start = start_ref[...]
    start = jnp.concatenate([start, start], axis=1)

    def step(j, carry):
        peak, total, acc = carry
        at_key = pl.ds(pl.multiple_of(j * BLOCK, BLOCK), BLOCK)
        s = dot(k_ref[0, at_key, :], qs, 1, 0)
        s = jnp.where(mask_of(start, j, i, bq), s, NEG)
        new = jnp.maximum(peak, jnp.max(s, axis=0, keepdims=True))
        p = jnp.exp(s - new)
        scale = jnp.exp(peak - new)
        total = total * scale + jnp.sum(p, axis=0, keepdims=True)
        acc = acc * scale + dot(v_ref[:, at_key], p.astype(BF16), 1, 0)
        return new, total, acc

    peak, total, acc = lax.fori_loop(
        low[i],
        i + 1,
        step,
        (
            jnp.full((1, 2 * bq), NEG, F32),
            jnp.zeros((1, 2 * bq), F32),
            jnp.zeros((HEAD_SIZE, 2 * bq), F32),
        ),
    )
    out = (acc / total).astype(BF16)
    o_ref[...] = jnp.concatenate([out[:, :bq], out[:, bq:]], axis=0)
    lse = peak + jnp.log(total)
    lse_ref[0] = jnp.concatenate([lse[:, :bq], lse[:, bq:]], axis=0)


def attend(q_t, k, v_t, start, low):
    rows = q_t.shape[1]
    heads = k.shape[0]
    blocks = rows // BLOCK
    return pl.pallas_call(
        attend_kernel,
        grid_spec=pltpu.PrefetchScalarGridSpec(
            num_scalar_prefetch=1,
            grid=(heads, blocks),
            in_specs=[
                pl.BlockSpec((2 * HEAD_SIZE, BLOCK), lambda h, i, low: (h, i)),
                pl.BlockSpec((1, rows, HEAD_SIZE), lambda h, i, low: (h, 0, 0)),
                pl.BlockSpec((HEAD_SIZE, rows), lambda h, i, low: (h, 0)),
                pl.BlockSpec((1, BLOCK), lambda h, i, low: (0, i)),
            ],
            out_specs=[
                pl.BlockSpec((2 * HEAD_SIZE, BLOCK), lambda h, i, low: (h, i)),
                pl.BlockSpec((1, 2, BLOCK), lambda h, i, low: (h, 0, i)),
            ],
        ),
        out_shape=[
            jax.ShapeDtypeStruct(q_t.shape, BF16),
            jax.ShapeDtypeStruct((heads, 2, rows), F32),
        ],
        cost_estimate=KERNEL_COST,
        name="attend",
    )(low, q_t, k, v_t, start)


def attend_back_kernel(
    low, q_ref, do_ref, o_ref, lse_ref, k_ref, v_ref, kt_ref, start_ref, cos_ref, sin_ref,
    dq_ref, dk_ref, dv_ref,
):
    i = pl.program_id(1)
    bq = BLOCK

    @pl.when(i == 0)
    def _():
        dk_ref[...] = jnp.zeros_like(dk_ref)
        dv_ref[...] = jnp.zeros_like(dv_ref)

    def side(a):
        return jnp.concatenate([a[:HEAD_SIZE], a[HEAD_SIZE:]], axis=1)

    qs = side(q_ref[...])
    dos = side(do_ref[...])
    inner = jnp.sum(dos.astype(F32) * side(o_ref[...]).astype(F32), axis=0, keepdims=True)
    lse = lse_ref[0]
    lse = jnp.concatenate([lse[0:1], lse[1:2]], axis=1)
    start = start_ref[...]
    start = jnp.concatenate([start, start], axis=1)

    def step(j, dq):
        at_key = pl.ds(pl.multiple_of(j * BLOCK, BLOCK), BLOCK)
        s = dot(k_ref[0, at_key, :], qs, 1, 0)
        p = jnp.where(mask_of(start, j, i, bq), jnp.exp(s - lse), 0.0)
        dp = dot(v_ref[0, at_key, :], dos, 1, 0)
        ds = (p * (dp - inner)).astype(BF16)
        dv_ref[0, at_key, :] += dot(p.astype(BF16), dos, 1, 1)
        dk_ref[0, at_key, :] += dot(ds, qs, 1, 1)
        return dq + dot(kt_ref[:, at_key], ds, 1, 0)

    dq = lax.fori_loop(low[i], i + 1, step, jnp.zeros((HEAD_SIZE, 2 * bq), F32))
    dq = dq * HEAD_SIZE ** (-0.5)
    cosine, sine = cos_ref[...], sin_ref[...]
    for h in range(2):
        one = dq[:HALF, h * bq : (h + 1) * bq]
        two = dq[HALF:, h * bq : (h + 1) * bq]
        dq_ref[h * HEAD_SIZE : h * HEAD_SIZE + HALF, :] = (one * cosine + two * sine).astype(BF16)
        dq_ref[h * HEAD_SIZE + HALF : (h + 1) * HEAD_SIZE, :] = (
            two * cosine - one * sine
        ).astype(BF16)


def attend_back(first, heads, q_t, do_t, o_t, lse, k, v, k_t, start, cosine, sine, low):
    rows = q_t.shape[1]
    blocks = rows // BLOCK
    pair = pl.BlockSpec((2 * HEAD_SIZE, BLOCK), lambda h, i, low: (h + first, i))
    whole = pl.BlockSpec((1, rows, HEAD_SIZE), lambda h, i, low: (h + first, 0, 0))
    table = pl.BlockSpec((HALF, BLOCK), lambda h, i, low: (0, i))
    grad = pl.BlockSpec((1, rows, HEAD_SIZE), lambda h, i, low: (h, 0, 0))
    return pl.pallas_call(
        attend_back_kernel,
        grid_spec=pltpu.PrefetchScalarGridSpec(
            num_scalar_prefetch=1,
            grid=(heads, blocks),
            in_specs=[
                pair,
                pair,
                pair,
                pl.BlockSpec((1, 2, BLOCK), lambda h, i, low: (h + first, 0, i)),
                whole,
                whole,
                pl.BlockSpec((HEAD_SIZE, rows), lambda h, i, low: (h + first, 0)),
                pl.BlockSpec((1, BLOCK), lambda h, i, low: (0, i)),
                table,
                table,
            ],
            out_specs=[
                pl.BlockSpec((2 * HEAD_SIZE, BLOCK), lambda h, i, low: (h, i)), grad, grad,
            ],
        ),
        out_shape=[
            jax.ShapeDtypeStruct((heads * 2 * HEAD_SIZE, rows), BF16),
            jax.ShapeDtypeStruct((heads, rows, HEAD_SIZE), F32),
            jax.ShapeDtypeStruct((heads, rows, HEAD_SIZE), F32),
        ],
        cost_estimate=KERNEL_COST,
        name="attend_back",
    )(low, q_t, do_t, o_t, lse, k, v, k_t, start, cosine, sine)


def pieces_of(rows, most):
    return [(r, min(most, rows - r)) for r in range(0, rows, most)]


def expert_kernel(
    table, count, parity, x_hbm, c_hbm, gate_ref, w_ref, keep_ref, send_ref, out_hbm, dx_hbm,
    dg_ref, mark_ref, xs, cs, oacc, dacc, xg, cg, xb, cb, dab, hgb, sems,
):
    e = pl.program_id(0)
    last = pl.num_programs(0) - 1
    rows, width = x_hbm.shape
    lanes = width // 128
    dp, rs, ff = w_ref.shape[0], w_ref.shape[3], w_ref.shape[4]
    stages = (xb, cb, dab)

    @pl.when(e == 0)
    def _():
        jobs = [
            (source.at[pl.ds(r, n), :], target, r, n)
            for source, target in ((x_hbm, xs), (c_hbm, cs))
            for r, n in pieces_of(rows, CAP)
        ]
        copies = [
            pltpu.make_async_copy(
                source, stages[i % 3].at[pl.ds(0, n), :], sems.at[i % 3]
            )
            for i, (source, _, _, n) in enumerate(jobs)
        ]
        for op in copies[:3]:
            op.start()
        oacc[...] = jnp.zeros_like(oacc)
        dacc[...] = jnp.zeros_like(dacc)
        xg[...] = jnp.zeros_like(xg)
        cg[...] = jnp.zeros_like(cg)
        for i, (_, target, r, n) in enumerate(jobs):
            copies[i].wait()
            for j in range(lanes):
                target[pl.ds(r * lanes + j, n, stride=lanes), :] = stages[i % 3][
                    :n, j * 128 : (j + 1) * 128
                ].astype(F32)
            if i + 3 < len(jobs):
                copies[i + 3].start()
        for target in (xs, cs):
            target[rows * lanes :, :] = jnp.zeros((8 * lanes, 128), F32)

    named = count[e]
    w_gate = w_ref[:, 0, 0].reshape(dp * rs, ff)
    w_up = w_ref[:, 0, 1].reshape(dp * rs, ff)
    w_low = w_ref[:, 0, 2, : rs // 2].reshape(dp * rs // 2, ff)
    w_high = w_ref[:, 0, 2, rs // 2 :].reshape(dp * rs // 2, ff)

    for t in range(CAP // TILE):
        here = slice(t * TILE, (t + 1) * TILE)

        @pl.when(named > t * TILE)
        def _(t=t, here=here):
            groups = (jnp.minimum(named - t * TILE, TILE) + STEP - 1) // STEP
            first = e * CAP + t * TILE

            def places(b):
                return [
                    pl.ds(pl.multiple_of(table[first + b * STEP + k], 8), lanes)
                    for k in range(STEP)
                ]

            def own(b):
                return [
                    pl.ds(pl.multiple_of(b * (STEP * lanes) + k * lanes, 8), lanes)
                    for k in range(STEP)
                ]

            def pick(b, carry):
                there, here_ = places(b), own(b)
                xrows = [xs[p, :] for p in there]
                crows = [cs[p, :] for p in there]
                for p, v, w in zip(here_, xrows, crows):
                    xg[p, :] = v
                    cg[p, :] = w
                return carry

            lax.fori_loop(0, groups, pick, 0)
            for j in range(lanes):
                one = slice(j * 128, (j + 1) * 128)
                xb[here, one] = xg[pl.ds(j, TILE, stride=lanes), :].astype(BF16)
                cb[here, one] = cg[pl.ds(j, TILE, stride=lanes), :].astype(BF16)
            gate = gate_ref[0, here, :]
            x = xb[here, :]
            c = cb[here, :]
            a = dot(x, w_gate, 1, 0)
            b = dot(x, w_up, 1, 0)
            sig = jax.nn.sigmoid(a)
            silu = a * sig
            hid = silu * b
            hg = (hid * gate).astype(BF16)
            hgb[here, :] = hg
            u = dot(c[:, :ff], w_low, 1, 1) + dot(c[:, ff:], w_high, 1, 1)
            dg_ref[0, here, :] = jnp.sum(hid * u, axis=1, keepdims=True)
            du = gate * u
            da = (du * b * sig * (1.0 + a * (1.0 - sig))).astype(BF16)
            db = (du * silu).astype(BF16)
            dab[here, :ff] = da
            dab[here, ff:] = db
            for half, w in enumerate((w_low, w_high)):
                y = dot(hg, w, 1, 0)
                for j in range(ff // 128):
                    xg[pl.ds(half * (ff // 128) + j, TILE, stride=lanes), :] = y[
                        :, j * 128 : (j + 1) * 128
                    ]
            dx = dot(da, w_gate, 1, 1) + dot(db, w_up, 1, 1)
            for j in range(lanes):
                cg[pl.ds(j, TILE, stride=lanes), :] = dx[:, j * 128 : (j + 1) * 128]

            def add(b, carry):
                there, here_ = places(b), own(b)
                outs = [oacc[p, :] + xg[q, :] for p, q in zip(there, here_)]
                backs = [dacc[p, :] + cg[q, :] for p, q in zip(there, here_)]
                for p, v, w in zip(there, outs, backs):
                    oacc[p, :] = v
                    dacc[p, :] = w
                return carry

            lax.fori_loop(0, groups, add, 0)

    even = parity[0] == 0

    def split(value, slot, low, high):
        v = value.reshape(dp // 2, 2, high - low, ff)
        first, second = v[:, 0], v[:, 1]
        keep_ref[:, 0, slot, low:high, :] = jnp.where(even, first, second)
        send_ref[:, 0, slot, low:high, :] = jnp.where(even, second, first)

    def grads(depth):
        x = xb[:depth, :]
        d = dab[:depth, :]
        split(dot(x, d[:, :ff], 0, 0).astype(BF16), 0, 0, rs)
        split(dot(x, d[:, ff:], 0, 0).astype(BF16), 1, 0, rs)
        h = hgb[:depth, :]
        c = cb[:depth, :]
        split(dot(h, c[:, :ff], 0, 0).astype(BF16), 2, 0, rs // 2)
        split(dot(h, c[:, ff:], 0, 0).astype(BF16), 2, rs // 2, rs)

    @pl.when(named == 0)
    def _():
        keep_ref[...] = jnp.zeros_like(keep_ref)
        send_ref[...] = jnp.zeros_like(send_ref)

    for t in range(CAP // TILE):

        @pl.when((named > t * TILE) & (named <= (t + 1) * TILE))
        def _(t=t):
            grads((t + 1) * TILE)

    @pl.when(e == last)
    def _():
        mark_ref[...] = jnp.zeros_like(mark_ref)
        jobs = [
            (source, target.at[pl.ds(r, n), :], r, n)
            for source, target in ((oacc, out_hbm), (dacc, dx_hbm))
            for r, n in pieces_of(rows, CAP)
        ]
        copies = [
            pltpu.make_async_copy(
                stages[i % 3].at[pl.ds(0, n), :], target, sems.at[i % 3]
            )
            for i, (_, target, _, n) in enumerate(jobs)
        ]
        for i, (source, _, r, n) in enumerate(jobs):
            if i >= 3:
                copies[i - 3].wait()
            for j in range(lanes):
                stages[i % 3][:n, j * 128 : (j + 1) * 128] = source[
                    pl.ds(r * lanes + j, n, stride=lanes), :
                ].astype(BF16)
            copies[i].start()
        for op in copies[-3:]:
            op.wait()


def expert_call(table, count, parity, x, c, gates, weights, first_expert, expert_count):
    rows, width = x.shape
    dp, _, _, rs, ff = weights.shape
    lanes = width // 128
    grads = pl.BlockSpec((dp // 2, 1, 3, rs, ff), lambda e, *_: (0, e, 0, 0, 0))
    hbm = pl.BlockSpec(memory_space=pl.ANY)
    return pl.pallas_call(
        expert_kernel,
        grid_spec=pltpu.PrefetchScalarGridSpec(
            num_scalar_prefetch=3,
            grid=(expert_count,),
            in_specs=[
                hbm,
                hbm,
                pl.BlockSpec((1, CAP, 1), lambda e, *_: (e + first_expert, 0, 0)),
                pl.BlockSpec(
                    (dp, 1, 3, rs, ff), lambda e, *_: (0, e + first_expert, 0, 0, 0)
                ),
            ],
            out_specs=[
                grads, grads, hbm, hbm, pl.BlockSpec((1, CAP, 1), lambda e, *_: (e, 0, 0)),
                pl.BlockSpec((8, 128), lambda e, *_: (0, 0)),
            ],
            scratch_shapes=[
                pltpu.VMEM(((rows + 8) * lanes, 128), F32),
                pltpu.VMEM(((rows + 8) * lanes, 128), F32),
                pltpu.VMEM(((rows + 8) * lanes, 128), F32),
                pltpu.VMEM(((rows + 8) * lanes, 128), F32),
                pltpu.VMEM((TILE * lanes, 128), F32),
                pltpu.VMEM((TILE * lanes, 128), F32),
                pltpu.VMEM((CAP, width), BF16),
                pltpu.VMEM((CAP, width), BF16),
                pltpu.VMEM((CAP, 2 * ff), BF16),
                pltpu.VMEM((CAP, ff), BF16),
                pltpu.SemaphoreType.DMA((3,)),
            ],
        ),
        out_shape=[
            jax.ShapeDtypeStruct((dp // 2, expert_count, 3, rs, ff), BF16),
            jax.ShapeDtypeStruct((dp // 2, expert_count, 3, rs, ff), BF16),
            jax.ShapeDtypeStruct((rows, width), BF16),
            jax.ShapeDtypeStruct((rows, width), BF16),
            jax.ShapeDtypeStruct((expert_count, CAP, 1), F32),
            jax.ShapeDtypeStruct((8, 128), F32),
        ],
        compiler_params=pltpu.CompilerParams(vmem_limit_bytes=63 * 2**20),
        cost_estimate=KERNEL_COST,
        name="experts",
    )(table, count, parity, x, c, gates, weights)


def shards(
    tokens, lengths, routes, norm1_gain, w_query, key_projection, value_projection, w_out,
    norm2_gain, w_router, w_gate, w_up, w_down, cotangent,
):
    tensor = lax.axis_size("tensor")
    rank = lax.axis_index("tensor")
    dp = lax.axis_size("dp")
    me = lax.axis_index("dp")
    local_rows, width = tokens.shape
    rows = local_rows * tensor
    heads = QUERY_HEADS // tensor
    kv_heads = KEY_VALUE_HEADS // tensor
    expert_local = w_gate.shape[0]
    shard_rows = norm1_gain.shape[0]
    own_row = rank * local_rows

    pack = jnp.concatenate(
        [
            w_query, key_projection, value_projection, w_out.T, w_router,
            norm1_gain[:, None], norm2_gain[:, None],
        ],
        axis=1,
    )
    used = pack.shape[1]
    pack = jnp.pad(pack, ((0, 0), (0, -used % 128)))
    small = gather_dp(pack).reshape(dp * shard_rows, pack.shape[1])
    d_qkv = w_query.shape[1] + 2 * key_projection.shape[1]
    d_q, d_k = w_query.shape[1], key_projection.shape[1]
    d_o = w_out.shape[0]
    qkv_weight = small[:, :d_qkv]
    out_weight_t = small[:, d_qkv : d_qkv + d_o]
    router_weight = small[:, d_qkv + d_o : d_qkv + d_o + EXPERTS]
    gains = small[:, used - 2 : used].astype(F32).T
    gain_one, gain_two = gains[0], gains[1]

    ff = w_gate.shape[2]
    down = jnp.concatenate([w_down[:, :, :ff], w_down[:, :, ff:]], axis=1)
    big_shard = jnp.stack([w_gate, w_up, down], axis=1)
    big = lax.all_gather(big_shard.reshape(-1, ff), "dp", axis=0, tiled=True)
    big = big.reshape((dp,) + big_shard.shape)

    inputs_all = gather_rows(tokens)
    grad_all = gather_rows(cotangent)

    seq = lengths[0]
    order = jnp.arange(seq.shape[0], dtype=jnp.int32)
    ends = jnp.sum(jnp.where(order[:, None] <= order[None, :], seq[:, None], 0), axis=0)
    row_index = jnp.arange(rows, dtype=jnp.int32)
    passed = row_index[None, :] >= ends[:, None]
    first_row = jnp.max(jnp.where(passed, ends[:, None], 0), axis=0)
    position = row_index - first_row
    frequency = 10000.0 ** (-2.0 * jnp.arange(HALF, dtype=F32) / HEAD_SIZE)
    angles = frequency[:, None] * position.astype(F32)[None, :]
    cosine, sine = jnp.cos(angles), jnp.sin(angles)
    low = first_row[::BLOCK] // BLOCK
    start = first_row[None, :]

    names = rank * expert_local + jnp.arange(expert_local, dtype=jnp.int32)
    member_all = jnp.any(
        routes[:, :, None] == jnp.arange(EXPERTS, dtype=jnp.int32)[None, None, :], axis=1
    )
    member = jnp.any(routes.T[None, :, :] == names[:, None, None], axis=1)
    count = jnp.sum(member.astype(jnp.int32), axis=1)
    table = jnp.sort(jnp.where(member, row_index[None, :], rows), axis=1)[:, :CAP]
    filled = jnp.arange(CAP, dtype=jnp.int32)[None, :] < count[:, None]

    normed_all, inverse_all = rms_norm(inputs_all.astype(F32), gain_one)
    hidden_one = normed_all.astype(BF16)
    qkv = dot(qkv_weight, hidden_one, 0, 1)
    q_t = (rope_t(qkv[:d_q], cosine, sine).astype(BF16).astype(F32) * HEAD_SIZE ** (-0.5)).astype(
        BF16
    )
    k_t = rope_t(qkv[d_q : d_q + d_k], cosine, sine).astype(BF16)
    v_t = qkv[d_q + d_k :].astype(BF16)
    k = jnp.transpose(k_t.reshape(kv_heads, HEAD_SIZE, rows), (0, 2, 1))
    v = jnp.transpose(v_t.reshape(kv_heads, HEAD_SIZE, rows), (0, 2, 1))
    o_t, lse = attend(q_t, k, v_t, start, low)
    inputs_f = tokens.astype(F32)
    residual_two = inputs_f + scatter_rows(dot(o_t, out_weight_t, 0, 1).astype(BF16))

    normed_two, inverse_two = rms_norm(residual_two, gain_two)
    hidden_rows = normed_two.astype(BF16)
    hidden_two = gather_rows(hidden_rows)
    logits = jnp.where(member_all, dot(hidden_two, router_weight, 1, 0), NEG)
    gates_f = jax.nn.softmax(logits, axis=-1)
    share = lax.dynamic_slice_in_dim(gates_f, rank * expert_local, expert_local, 1)
    share_t = share.astype(BF16).astype(F32).T
    slot_gate = jnp.sum(
        jnp.where(table[:, :, None] == row_index[None, None, :], share_t[:, None, :], 0.0), axis=2
    )[:, :, None]

    calls = EXPERT_CALLS
    each = expert_local // calls
    parity = (me % 2).astype(jnp.int32).reshape(1)
    slots = table * (width // 128)
    out_part, dx_part = 0.0, 0.0
    dg, sums = [], []
    for call in range(calls):
        picked = slice(call * each, (call + 1) * each)
        made = []

        def work(counted, picked=picked, call=call, made=made):
            *outs, mark = expert_call(
                slots[picked].reshape(-1), counted, parity, hidden_two, grad_all, slot_gate,
                big, call * each, each,
            )
            made.extend(outs)
            return [mark]

        phase(work, [count[picked]], sums)
        keep, send, out_p, dx_p, dg_p = made
        sums.append(Reduce(keep, send))
        out_part = out_part + out_p.astype(F32)
        dx_part = dx_part + dx_p.astype(F32)
        dg.append(dg_p[:, :, 0])

    dg = jnp.where(filled, jnp.concatenate(dg, axis=0), 0.0)

    def over_x(sent, sent_out, dg):
        dg = jnp.sum(
            jnp.where(table[:, None, :] == row_index[None, :, None], dg[:, None, :], 0.0), axis=2
        )
        d_dense = lax.dynamic_update_slice_in_dim(
            jnp.zeros((rows, EXPERTS), F32), dg.T, rank * expert_local, 1
        )
        return [scatter_rows(sent), scatter_rows(d_dense), sent_out]

    d_rows, d_gates, out_part = phase(
        over_x, [dx_part.astype(BF16), out_part.astype(BF16), dg], sums[1:]
    )
    gates_own = lax.dynamic_slice_in_dim(gates_f, own_row, local_rows, 0)
    d_logits = gates_own * (d_gates - jnp.sum(d_gates * gates_own, axis=-1, keepdims=True))
    router_grad = jnp.dot(hidden_rows.astype(F32).T, d_logits, precision=exact_mode)
    d_rows = d_rows + jnp.dot(d_logits, router_weight.astype(F32).T, precision=exact_mode)
    d_norm_two, gain_two_grad = rms_back(d_rows, residual_two, inverse_two, gain_two)
    d_residual = cotangent.astype(F32) + d_norm_two
    (d_all,) = phase(
        lambda sent: [gather_rows(sent)], [d_residual.astype(BF16)], sums[2:]
    )

    do_t = dot(out_weight_t, d_all, 0, 1).astype(BF16)

    def back(do_t, out_part):
        parts = attend_back(
            0, kv_heads, q_t, do_t, o_t, lse, k, v, k_t, start, cosine, sine, low
        )
        return list(parts) + [scatter_rows(out_part)]

    dq_t, dk, dv, moe_rows = phase(back, [do_t, out_part], sums[3:])
    output = (residual_two + moe_rows).astype(BF16)
    dk_t = rope_t(jnp.transpose(dk, (0, 2, 1)).reshape(d_k, rows), cosine, -sine).astype(BF16)
    dv_t = jnp.transpose(dv, (0, 2, 1)).reshape(d_k, rows).astype(BF16)
    d_qkv_t = jnp.concatenate([dq_t, dk_t, dv_t], axis=0)
    grad_out_t = dot(d_all, o_t, 0, 1).astype(BF16)
    grad_qkv = dot(hidden_one, d_qkv_t, 0, 1).astype(BF16)
    d_hidden_part = dot(d_qkv_t, qkv_weight, 0, 1)
    gain_one_grad = jnp.sum(d_hidden_part * inputs_all.astype(F32) * inverse_all, axis=0)
    misc = jnp.concatenate(
        [router_grad, gain_one_grad[:, None], gain_two_grad[:, None]], axis=1
    ).astype(BF16)
    misc = jnp.pad(misc, ((0, 0), (0, -misc.shape[1] % 128)))
    small_grad = jnp.concatenate([grad_qkv, grad_out_t, misc], axis=1)
    small_grad = small_grad.reshape(dp // 2, 2, shard_rows, small_grad.shape[1])
    even = parity[0] == 0
    first, second = small_grad[:, 0], small_grad[:, 1]
    small = Reduce(jnp.where(even, first, second), jnp.where(even, second, first))
    d_hidden_one = scatter_rows(d_hidden_part.astype(BF16))
    for _ in range(3):
        small.take(small.move(small.sends()))
    small_sum = small.result()
    d_norm_one, _ = rms_back(
        d_hidden_one, inputs_f, lax.dynamic_slice_in_dim(inverse_all, own_row, local_rows, 0),
        gain_one,
    )
    grad_tokens = (d_residual + d_norm_one).astype(BF16)

    total = jnp.concatenate([r.result() for r in sums], axis=0)
    grad_gate, grad_up = total[:, 0], total[:, 1]
    half = shard_rows // 2
    grad_down = jnp.concatenate([total[:, 2, :half], total[:, 2, half:]], axis=2)
    over_tensor = small_sum[:, d_qkv + d_o : used]
    if tensor == 2:
        over_tensor = over_tensor + lax.ppermute(over_tensor, "tensor", [(0, 1), (1, 0)])
    else:
        over_tensor = lax.psum(over_tensor, "tensor")
    return (
        output,
        grad_tokens,
        over_tensor[:, EXPERTS],
        small_sum[:, :d_q],
        small_sum[:, d_q : d_q + d_k],
        small_sum[:, d_q + d_k : d_qkv],
        small_sum[:, d_qkv : d_qkv + d_o].T,
        over_tensor[:, EXPERTS + 1],
        over_tensor[:, :EXPERTS],
        grad_gate,
        grad_up,
        grad_down,
    )


def solution(mesh):
    return jax.shard_map(
        shards,
        mesh=mesh,
        in_specs=(
            P(("dp", "tensor"), None),
            P("dp", None),
            P("dp", None),
            P("dp"),
            P("dp", "tensor"),
            P("dp", "tensor"),
            P("dp", "tensor"),
            P("tensor", "dp"),
            P("dp"),
            P("dp", None),
            P("tensor", "dp", None),
            P("tensor", "dp", None),
            P("tensor", "dp", None),
            P(("dp", "tensor"), None),
        ),
        out_specs=(
            P(("dp", "tensor"), None),
            P(("dp", "tensor"), None),
            P("dp"),
            P("dp", "tensor"),
            P("dp", "tensor"),
            P("dp", "tensor"),
            P("tensor", "dp"),
            P("dp"),
            P("dp", None),
            P("tensor", "dp", None),
            P("tensor", "dp", None),
            P("tensor", "dp", None),
        ),
        check_vma=False,
    )
```

```python
import functools

import jax
import jax.numpy as jnp
from jax import lax
from jax.experimental import pallas as pl
from jax.experimental.pallas import tpu as pltpu
from jax.sharding import PartitionSpec as P

QUERY_HEADS = 16
KEY_VALUE_HEADS = 8
HEAD_SIZE = 64
HALF = HEAD_SIZE // 2
EXPERTS = 32
CAP = 768
TILE = 256
BLOCK = 256
STEP = 16
EXPERT_CALLS = 4
KERNEL_COST = pl.CostEstimate(flops=1, bytes_accessed=150 * 10**6, transcendentals=0)

exact_mode = lax.Precision.HIGHEST
F32 = jnp.float32
BF16 = jnp.bfloat16
NEG = -1e30


def dot(a, b, ca, cb):
    return lax.dot_general(a, b, (((ca,), (cb,)), ((), ())), preferred_element_type=F32)


def z_core_shape(dp):
    return (4, 2, 2) if dp == 16 else None


def gather_rows(x, axis="tensor"):
    n = lax.axis_size(axis)
    if n != 2:
        return lax.all_gather(x, axis, axis=0, tiled=True)
    rank = lax.axis_index(axis)
    other = lax.ppermute(x, axis, [(0, 1), (1, 0)])
    first = rank == 0
    return jnp.concatenate([jnp.where(first, x, other), jnp.where(first, other, x)], axis=0)


def swap_rows(x):
    if lax.axis_size("tensor") != 2:
        return lax.all_gather(x, "tensor", axis=0, tiled=True)
    return lax.ppermute(x, "tensor", [(0, 1), (1, 0)])


def join_rows(x, swapped):
    if lax.axis_size("tensor") != 2:
        return swapped
    first = lax.axis_index("tensor") == 0
    return jnp.concatenate([jnp.where(first, x, swapped), jnp.where(first, swapped, x)], axis=0)


def scatter_rows(x, axis="tensor"):
    n = lax.axis_size(axis)
    rows = x.shape[0] // n
    if n != 2:
        return lax.psum_scatter(x, axis, scatter_dimension=0, tiled=True).astype(F32)
    rank = lax.axis_index(axis)
    sent = lax.ppermute(
        lax.dynamic_slice_in_dim(x, (1 - rank) * rows, rows, 0), axis, [(0, 1), (1, 0)]
    )
    own = lax.dynamic_slice_in_dim(x, rank * rows, rows, 0)
    return own.astype(F32) + sent.astype(F32)


def dp_pairs(move):
    pairs = []
    for z in range(4):
        for y in range(2):
            for c in range(2):
                tz, ty, tc = move(z, y, c)
                pairs.append((z * 4 + y * 2 + c, tz * 4 + ty * 2 + tc))
    return pairs


CORE_PAIRS = dp_pairs(lambda z, y, c: (z, y, 1 - c))
Y_PAIRS = dp_pairs(lambda z, y, c: (z, 1 - y, c))
Z_PAIRS = {k: dp_pairs(lambda z, y, c, k=k: ((z + k) % 4, y, c)) for k in (1, 2, 3)}


def place(own, index, parts):
    buf = jnp.zeros((len(parts) + 1,) + own.shape, own.dtype)
    for i, a in [(index, own)] + parts:
        buf = lax.dynamic_update_index_in_dim(buf, a, i, 0)
    return buf


def gather_dp(x):
    n = lax.axis_size("dp")
    if z_core_shape(n) is None:
        return lax.all_gather(x, "dp", axis=0, tiled=False)
    me = lax.axis_index("dp")
    z, y, c = me // 4, (me // 2) % 2, me % 2
    parts = [((z - k) % 4, lax.ppermute(x, "dp", Z_PAIRS[k])) for k in (1, 3, 2)]
    buf = place(x, z, parts)
    buf = place(buf, y, [(1 - y, lax.ppermute(buf, "dp", Y_PAIRS))])
    buf = place(buf, c, [(1 - c, lax.ppermute(buf, "dp", CORE_PAIRS))])
    return jnp.transpose(buf, (2, 1, 0) + tuple(range(3, buf.ndim))).reshape((n,) + x.shape)


def at(a, i, axis):
    return lax.dynamic_index_in_dim(a, i, axis, keepdims=False)


def line_place():
    me = lax.axis_index("dp")
    return me // 4, (me // 2) % 2


class Reduce:
    def __init__(self, keep, send):
        self.by_hand = z_core_shape(lax.axis_size("dp")) is not None
        self.keep, self.send = keep, send
        self.stage = 0

    def split(self, *sizes):
        if not self.by_hand or sum(sizes) != self.keep.shape[1]:
            return [self] + [None] * (len(sizes) - 1)
        parts = []
        for i, size in enumerate(sizes):
            run = slice(sum(sizes[:i]), sum(sizes[:i]) + size)
            part = Reduce(self.keep[:, run], None)
            part.core, part.stage = self.core[:, run], 1
            parts.append(part)
        return parts

    def sends(self):
        if not self.by_hand:
            return []
        if self.stage == 0:
            return [self.send]
        z, y = line_place()
        if self.stage == 1:
            self.keep = self.keep.reshape((4, 2) + self.keep.shape[1:])
            self.core = self.core.reshape(self.keep.shape)
            return [
                (
                    at(self.keep, 1 - y, 1).astype(F32) + at(self.core, 1 - y, 1).astype(F32)
                ).astype(BF16)
            ]

        def line(i):
            return (
                at(at(self.keep, y, 1), i, 0).astype(F32)
                + at(at(self.core, y, 1), i, 0).astype(F32)
                + at(self.over, i, 0).astype(F32)
            )

        self.own = line(z)
        return [line((z + k) % 4).astype(BF16) for k in (2, 1, 3)]

    def move(self, sent):
        if not self.by_hand:
            return []
        pairs = ([CORE_PAIRS], [Y_PAIRS], [Z_PAIRS[k] for k in (2, 1, 3)])[self.stage]
        return [lax.ppermute(a, "dp", p) for a, p in zip(sent, pairs)]

    def take(self, got):
        if self.by_hand:
            if self.stage == 0:
                (self.core,) = got
            elif self.stage == 1:
                (self.over,) = got
            else:
                self.parts = got
        self.stage += 1

    def result(self):
        n = lax.axis_size("dp")
        if not self.by_hand:
            even = lax.axis_index("dp") % 2 == 0
            first = jnp.where(even, self.keep, self.send)
            second = jnp.where(even, self.send, self.keep)
            both = jnp.stack([first, second], axis=1).reshape((n,) + self.keep.shape[1:])
            return lax.psum_scatter(both, "dp", scatter_dimension=0, tiled=False).astype(F32)
        total = self.own
        for a in self.parts:
            total = total + a.astype(F32)
        return total


def phase(work, inputs, reduces):
    reduces = [r for r in reduces if r is not None]
    sends = [r.sends() for r in reduces]
    (inputs, sends) = lax.optimization_barrier((list(inputs), sends))
    results = work(*inputs)
    moved = [r.move(sent) for r, sent in zip(reduces, sends)]
    results, moved = lax.optimization_barrier((results, moved))
    for r, got in zip(reduces, moved):
        r.take(got)
    return results


def rms_norm(values, gain):
    inverse = lax.rsqrt(jnp.mean(values * values, axis=-1, keepdims=True) + 1e-06)
    return (values * inverse * gain, inverse)


def rms_back(grad_rows, values, inverse, gain):
    scaled = grad_rows * gain
    gain_grad = jnp.sum(grad_rows * values * inverse, axis=0)
    inner = jnp.mean(scaled * values, axis=-1, keepdims=True)
    return (inverse * scaled - values * inverse * inverse * inverse * inner, gain_grad)


def rope_t(values, cosine, sine):
    rows = values.shape[1]
    v = values.reshape(-1, 2, HALF, rows)
    one, two = v[:, 0], v[:, 1]
    return jnp.stack(
        [one * cosine - two * sine, two * cosine + one * sine], axis=1
    ).reshape(values.shape)


def mask_of(start, j, i, bq):
    key = j * BLOCK + lax.broadcasted_iota(jnp.int32, (BLOCK, 2 * bq), 0)
    query = lax.broadcasted_iota(jnp.int32, (BLOCK, 2 * bq), 1)
    query = i * bq + jnp.where(query >= bq, query - bq, query)
    return (key >= start) & (key <= query)


def attend_kernel(low, q_ref, k_ref, v_ref, start_ref, o_ref, lse_ref):
    i = pl.program_id(1)
    bq = BLOCK
    q = q_ref[...]
    qs = jnp.concatenate([q[:HEAD_SIZE], q[HEAD_SIZE:]], axis=1)
    start = start_ref[...]
    start = jnp.concatenate([start, start], axis=1)

    def step(j, carry):
        peak, total, acc = carry
        at_key = pl.ds(pl.multiple_of(j * BLOCK, BLOCK), BLOCK)
        s = dot(k_ref[0, at_key, :], qs, 1, 0)
        s = jnp.where(mask_of(start, j, i, bq), s, NEG)
        new = jnp.maximum(peak, jnp.max(s, axis=0, keepdims=True))
        p = jnp.exp(s - new)
        scale = jnp.exp(peak - new)
        total = total * scale + jnp.sum(p, axis=0, keepdims=True)
        acc = acc * scale + dot(v_ref[:, at_key], p.astype(BF16), 1, 0)
        return new, total, acc

    peak, total, acc = lax.fori_loop(
        low[i],
        i + 1,
        step,
        (
            jnp.full((1, 2 * bq), NEG, F32),
            jnp.zeros((1, 2 * bq), F32),
            jnp.zeros((HEAD_SIZE, 2 * bq), F32),
        ),
    )
    out = (acc / total).astype(BF16)
    o_ref[...] = jnp.concatenate([out[:, :bq], out[:, bq:]], axis=0)
    lse = peak + jnp.log(total)
    lse_ref[0] = jnp.concatenate([lse[:, :bq], lse[:, bq:]], axis=0)


def attend(q_t, k, v_t, start, low):
    rows = q_t.shape[1]
    heads = k.shape[0]
    blocks = rows // BLOCK
    return pl.pallas_call(
        attend_kernel,
        grid_spec=pltpu.PrefetchScalarGridSpec(
            num_scalar_prefetch=1,
            grid=(heads, blocks),
            in_specs=[
                pl.BlockSpec((2 * HEAD_SIZE, BLOCK), lambda h, i, low: (h, i)),
                pl.BlockSpec((1, rows, HEAD_SIZE), lambda h, i, low: (h, 0, 0)),
                pl.BlockSpec((HEAD_SIZE, rows), lambda h, i, low: (h, 0)),
                pl.BlockSpec((1, BLOCK), lambda h, i, low: (0, i)),
            ],
            out_specs=[
                pl.BlockSpec((2 * HEAD_SIZE, BLOCK), lambda h, i, low: (h, i)),
                pl.BlockSpec((1, 2, BLOCK), lambda h, i, low: (h, 0, i)),
            ],
        ),
        out_shape=[
            jax.ShapeDtypeStruct(q_t.shape, BF16),
            jax.ShapeDtypeStruct((heads, 2, rows), F32),
        ],
        cost_estimate=KERNEL_COST,
        name="attend",
    )(low, q_t, k, v_t, start)


def attend_back_kernel(
    low, q_ref, do_ref, o_ref, lse_ref, k_ref, v_ref, kt_ref, start_ref, cos_ref, sin_ref,
    dq_ref, dk_ref, dv_ref, dk_sum, dv_sum,
):
    i = pl.program_id(1)
    bq = BLOCK

    @pl.when(i == 0)
    def _():
        dk_sum[...] = jnp.zeros_like(dk_sum)
        dv_sum[...] = jnp.zeros_like(dv_sum)

    def side(a):
        return jnp.concatenate([a[:HEAD_SIZE], a[HEAD_SIZE:]], axis=1)

    qs = side(q_ref[...])
    dos = side(do_ref[...])
    inner = jnp.sum(dos.astype(F32) * side(o_ref[...]).astype(F32), axis=0, keepdims=True)
    lse = lse_ref[0]
    lse = jnp.concatenate([lse[0:1], lse[1:2]], axis=1)
    start = start_ref[...]
    start = jnp.concatenate([start, start], axis=1)

    def step(j, dq):
        at_key = pl.ds(pl.multiple_of(j * BLOCK, BLOCK), BLOCK)
        s = dot(k_ref[0, at_key, :], qs, 1, 0)
        p = jnp.where(mask_of(start, j, i, bq), jnp.exp(s - lse), 0.0)
        dp = dot(v_ref[0, at_key, :], dos, 1, 0)
        ds = (p * (dp - inner)).astype(BF16)
        dv_sum[:, at_key] += dot(dos, p.astype(BF16), 1, 1)
        dk_sum[:, at_key] += dot(qs, ds, 1, 1)
        return dq + dot(kt_ref[:, at_key], ds, 1, 0)

    dq = lax.fori_loop(low[i], i + 1, step, jnp.zeros((HEAD_SIZE, 2 * bq), F32))
    dq = dq * HEAD_SIZE ** (-0.5)
    here = pl.ds(pl.multiple_of(i * bq, bq), bq)

    def turn_back(v, cosine, sine):
        one, two = v[:HALF], v[HALF:]
        return jnp.concatenate(
            [one * cosine + two * sine, two * cosine - one * sine], axis=0
        ).astype(BF16)

    for h in range(2):
        dq_ref[h * HEAD_SIZE : (h + 1) * HEAD_SIZE, :] = turn_back(
            dq[:, h * bq : (h + 1) * bq], cos_ref[:, here], sin_ref[:, here]
        )

    @pl.when(i == pl.num_programs(1) - 1)
    def _():
        dk_ref[...] = turn_back(dk_sum[...], cos_ref[...], sin_ref[...])
        dv_ref[...] = dv_sum[...].astype(BF16)


def attend_back(first, heads, q_t, do_t, o_t, lse, k, v, k_t, start, cosine, sine, low):
    rows = q_t.shape[1]
    blocks = rows // BLOCK
    pair = pl.BlockSpec((2 * HEAD_SIZE, BLOCK), lambda h, i, low: (h + first, i))
    whole = pl.BlockSpec((1, rows, HEAD_SIZE), lambda h, i, low: (h + first, 0, 0))
    table = pl.BlockSpec((HALF, rows), lambda h, i, low: (0, 0))
    grad = pl.BlockSpec((HEAD_SIZE, rows), lambda h, i, low: (h, 0))
    return pl.pallas_call(
        attend_back_kernel,
        grid_spec=pltpu.PrefetchScalarGridSpec(
            num_scalar_prefetch=1,
            grid=(heads, blocks),
            in_specs=[
                pair,
                pair,
                pair,
                pl.BlockSpec((1, 2, BLOCK), lambda h, i, low: (h + first, 0, i)),
                whole,
                whole,
                pl.BlockSpec((HEAD_SIZE, rows), lambda h, i, low: (h + first, 0)),
                pl.BlockSpec((1, BLOCK), lambda h, i, low: (0, i)),
                table,
                table,
            ],
            out_specs=[
                pl.BlockSpec((2 * HEAD_SIZE, BLOCK), lambda h, i, low: (h, i)), grad, grad,
            ],
            scratch_shapes=[
                pltpu.VMEM((HEAD_SIZE, rows), F32), pltpu.VMEM((HEAD_SIZE, rows), F32),
            ],
        ),
        out_shape=[
            jax.ShapeDtypeStruct((heads * 2 * HEAD_SIZE, rows), BF16),
            jax.ShapeDtypeStruct((heads * HEAD_SIZE, rows), BF16),
            jax.ShapeDtypeStruct((heads * HEAD_SIZE, rows), BF16),
        ],
        cost_estimate=KERNEL_COST,
        name="attend_back",
    )(low, q_t, do_t, o_t, lse, k, v, k_t, start, cosine, sine)


def pieces_of(rows, most):
    return [(r, min(most, rows - r)) for r in range(0, rows, most)]


def expert_kernel(
    table, count, parity, x_hbm, c_hbm, gate_ref, w_ref, keep_ref, send_ref, out_hbm, dx_hbm,
    dg_ref, mark_ref, xs, cs, oacc, dacc, xg, cg, xb, cb, dab, hgb, sems,
):
    e = pl.program_id(0)
    last = pl.num_programs(0) - 1
    rows, width = x_hbm.shape
    lanes = width // 128
    dp, rs, ff = w_ref.shape[0], w_ref.shape[3], w_ref.shape[4]
    stages = (xb, cb, dab)

    @pl.when(e == 0)
    def _():
        jobs = [
            (source.at[pl.ds(r, n), :], target, r, n)
            for source, target in ((x_hbm, xs), (c_hbm, cs))
            for r, n in pieces_of(rows, CAP)
        ]
        copies = [
            pltpu.make_async_copy(
                source, stages[i % 3].at[pl.ds(0, n), :], sems.at[i % 3]
            )
            for i, (source, _, _, n) in enumerate(jobs)
        ]
        for op in copies[:3]:
            op.start()
        oacc[...] = jnp.zeros_like(oacc)
        dacc[...] = jnp.zeros_like(dacc)
        xg[...] = jnp.zeros_like(xg)
        cg[...] = jnp.zeros_like(cg)
        for i, (_, target, r, n) in enumerate(jobs):
            copies[i].wait()
            for j in range(lanes):
                target[pl.ds(r * lanes + j, n, stride=lanes), :] = stages[i % 3][
                    :n, j * 128 : (j + 1) * 128
                ].astype(F32)
            if i + 3 < len(jobs):
                copies[i + 3].start()
        for target in (xs, cs):
            target[rows * lanes :, :] = jnp.zeros((8 * lanes, 128), F32)

    named = count[e]
    w_gate = w_ref[:, 0, 0].reshape(dp * rs, ff)
    w_up = w_ref[:, 0, 1].reshape(dp * rs, ff)
    w_low = w_ref[:, 0, 2, : rs // 2].reshape(dp * rs // 2, ff)
    w_high = w_ref[:, 0, 2, rs // 2 :].reshape(dp * rs // 2, ff)

    for t in range(CAP // TILE):
        here = slice(t * TILE, (t + 1) * TILE)

        @pl.when(named > t * TILE)
        def _(t=t, here=here):
            groups = (jnp.minimum(named - t * TILE, TILE) + STEP - 1) // STEP
            first = e * CAP + t * TILE

            def places(b):
                return [
                    pl.ds(pl.multiple_of(table[first + b * STEP + k], 8), lanes)
                    for k in range(STEP)
                ]

            def own(b):
                return [
                    pl.ds(pl.multiple_of(b * (STEP * lanes) + k * lanes, 8), lanes)
                    for k in range(STEP)
                ]

            def pick(b, carry):
                there, here_ = places(b), own(b)
                xrows = [xs[p, :] for p in there]
                crows = [cs[p, :] for p in there]
                for p, v, w in zip(here_, xrows, crows):
                    xg[p, :] = v
                    cg[p, :] = w
                return carry

            lax.fori_loop(0, groups, pick, 0)
            for j in range(lanes):
                one = slice(j * 128, (j + 1) * 128)
                xb[here, one] = xg[pl.ds(j, TILE, stride=lanes), :].astype(BF16)
                cb[here, one] = cg[pl.ds(j, TILE, stride=lanes), :].astype(BF16)
            gate = gate_ref[0, here, :]
            x = xb[here, :]
            c = cb[here, :]
            a = dot(x, w_gate, 1, 0)
            b = dot(x, w_up, 1, 0)
            sig = jax.nn.sigmoid(a)
            silu = a * sig
            hid = silu * b
            hg = (hid * gate).astype(BF16)
            hgb[here, :] = hg
            u = dot(c[:, :ff], w_low, 1, 1) + dot(c[:, ff:], w_high, 1, 1)
            dg_ref[0, here, :] = jnp.sum(hid * u, axis=1, keepdims=True)
            du = gate * u
            da = (du * b * sig * (1.0 + a * (1.0 - sig))).astype(BF16)
            db = (du * silu).astype(BF16)
            dab[here, :ff] = da
            dab[here, ff:] = db
            for half, w in enumerate((w_low, w_high)):
                y = dot(hg, w, 1, 0)
                for j in range(ff // 128):
                    xg[pl.ds(half * (ff // 128) + j, TILE, stride=lanes), :] = y[
                        :, j * 128 : (j + 1) * 128
                    ]
            dx = dot(da, w_gate, 1, 1) + dot(db, w_up, 1, 1)
            for j in range(lanes):
                cg[pl.ds(j, TILE, stride=lanes), :] = dx[:, j * 128 : (j + 1) * 128]

            def add(b, carry):
                there, here_ = places(b), own(b)
                outs = [oacc[p, :] + xg[q, :] for p, q in zip(there, here_)]
                backs = [dacc[p, :] + cg[q, :] for p, q in zip(there, here_)]
                for p, v, w in zip(there, outs, backs):
                    oacc[p, :] = v
                    dacc[p, :] = w
                return carry

            lax.fori_loop(0, groups, add, 0)

    even = parity[0] == 0

    def split(value, slot, low, high):
        v = value.reshape(dp // 2, 2, high - low, ff)
        first, second = v[:, 0], v[:, 1]
        keep_ref[:, 0, slot, low:high, :] = jnp.where(even, first, second)
        send_ref[:, 0, slot, low:high, :] = jnp.where(even, second, first)

    def grads(depth):
        x = xb[:depth, :]
        d = dab[:depth, :]
        split(dot(x, d[:, :ff], 0, 0).astype(BF16), 0, 0, rs)
        split(dot(x, d[:, ff:], 0, 0).astype(BF16), 1, 0, rs)
        h = hgb[:depth, :]
        c = cb[:depth, :]
        split(dot(h, c[:, :ff], 0, 0).astype(BF16), 2, 0, rs // 2)
        split(dot(h, c[:, ff:], 0, 0).astype(BF16), 2, rs // 2, rs)

    @pl.when(named == 0)
    def _():
        keep_ref[...] = jnp.zeros_like(keep_ref)
        send_ref[...] = jnp.zeros_like(send_ref)

    for t in range(CAP // TILE):

        @pl.when((named > t * TILE) & (named <= (t + 1) * TILE))
        def _(t=t):
            grads((t + 1) * TILE)

    @pl.when(e == last)
    def _():
        mark_ref[...] = jnp.zeros_like(mark_ref)
        jobs = [
            (source, target.at[pl.ds(r, n), :], r, n)
            for source, target in ((oacc, out_hbm), (dacc, dx_hbm))
            for r, n in pieces_of(rows, CAP)
        ]
        copies = [
            pltpu.make_async_copy(
                stages[i % 3].at[pl.ds(0, n), :], target, sems.at[i % 3]
            )
            for i, (_, target, _, n) in enumerate(jobs)
        ]
        for i, (source, _, r, n) in enumerate(jobs):
            if i >= 3:
                copies[i - 3].wait()
            for j in range(lanes):
                stages[i % 3][:n, j * 128 : (j + 1) * 128] = source[
                    pl.ds(r * lanes + j, n, stride=lanes), :
                ].astype(BF16)
            copies[i].start()
        for op in copies[-3:]:
            op.wait()


def expert_call(table, count, parity, x, c, gates, weights, first_expert, expert_count):
    rows, width = x.shape
    dp, _, _, rs, ff = weights.shape
    lanes = width // 128
    grads = pl.BlockSpec((dp // 2, 1, 3, rs, ff), lambda e, *_: (0, e, 0, 0, 0))
    hbm = pl.BlockSpec(memory_space=pl.ANY)
    return pl.pallas_call(
        expert_kernel,
        grid_spec=pltpu.PrefetchScalarGridSpec(
            num_scalar_prefetch=3,
            grid=(expert_count,),
            in_specs=[
                hbm,
                hbm,
                pl.BlockSpec((1, CAP, 1), lambda e, *_: (e + first_expert, 0, 0)),
                pl.BlockSpec(
                    (dp, 1, 3, rs, ff), lambda e, *_: (0, e + first_expert, 0, 0, 0)
                ),
            ],
            out_specs=[
                grads, grads, hbm, hbm, pl.BlockSpec((1, CAP, 1), lambda e, *_: (e, 0, 0)),
                pl.BlockSpec((8, 128), lambda e, *_: (0, 0)),
            ],
            scratch_shapes=[
                pltpu.VMEM(((rows + 8) * lanes, 128), F32),
                pltpu.VMEM(((rows + 8) * lanes, 128), F32),
                pltpu.VMEM(((rows + 8) * lanes, 128), F32),
                pltpu.VMEM(((rows + 8) * lanes, 128), F32),
                pltpu.VMEM((TILE * lanes, 128), F32),
                pltpu.VMEM((TILE * lanes, 128), F32),
                pltpu.VMEM((CAP, width), BF16),
                pltpu.VMEM((CAP, width), BF16),
                pltpu.VMEM((CAP, 2 * ff), BF16),
                pltpu.VMEM((CAP, ff), BF16),
                pltpu.SemaphoreType.DMA((3,)),
            ],
        ),
        out_shape=[
            jax.ShapeDtypeStruct((dp // 2, expert_count, 3, rs, ff), BF16),
            jax.ShapeDtypeStruct((dp // 2, expert_count, 3, rs, ff), BF16),
            jax.ShapeDtypeStruct((rows, width), BF16),
            jax.ShapeDtypeStruct((rows, width), BF16),
            jax.ShapeDtypeStruct((expert_count, CAP, 1), F32),
            jax.ShapeDtypeStruct((8, 128), F32),
        ],
        compiler_params=pltpu.CompilerParams(vmem_limit_bytes=63 * 2**20),
        cost_estimate=KERNEL_COST,
        name="experts",
    )(table, count, parity, x, c, gates, weights)


def shards(
    tokens, lengths, routes, norm1_gain, w_query, key_projection, value_projection, w_out,
    norm2_gain, w_router, w_gate, w_up, w_down, cotangent,
):
    tensor = lax.axis_size("tensor")
    rank = lax.axis_index("tensor")
    dp = lax.axis_size("dp")
    me = lax.axis_index("dp")
    local_rows, width = tokens.shape
    rows = local_rows * tensor
    heads = QUERY_HEADS // tensor
    kv_heads = KEY_VALUE_HEADS // tensor
    expert_local = w_gate.shape[0]
    shard_rows = norm1_gain.shape[0]
    own_row = rank * local_rows

    pack = jnp.concatenate(
        [
            w_query, key_projection, value_projection, w_out.T, w_router,
            norm1_gain[:, None], norm2_gain[:, None],
        ],
        axis=1,
    )
    used = pack.shape[1]
    pack = jnp.pad(pack, ((0, 0), (0, -used % 128)))
    small = gather_dp(pack).reshape(dp * shard_rows, pack.shape[1])
    d_qkv = w_query.shape[1] + 2 * key_projection.shape[1]
    d_q, d_k = w_query.shape[1], key_projection.shape[1]
    d_o = w_out.shape[0]
    qkv_weight = small[:, :d_qkv]
    out_weight_t = small[:, d_qkv : d_qkv + d_o]
    router_weight = small[:, d_qkv + d_o : d_qkv + d_o + EXPERTS]
    gains = small[:, used - 2 : used].astype(F32).T
    gain_one, gain_two = gains[0], gains[1]

    ff = w_gate.shape[2]
    down = jnp.concatenate([w_down[:, :, :ff], w_down[:, :, ff:]], axis=1)
    big_shard = jnp.stack([w_gate, w_up, down], axis=1)
    big = lax.all_gather(big_shard.reshape(-1, ff), "dp", axis=0, tiled=True)
    big = big.reshape((dp,) + big_shard.shape)

    inputs_all = gather_rows(tokens)

    seq = lengths[0]
    order = jnp.arange(seq.shape[0], dtype=jnp.int32)
    ends = jnp.sum(jnp.where(order[:, None] <= order[None, :], seq[:, None], 0), axis=0)
    row_index = jnp.arange(rows, dtype=jnp.int32)
    passed = row_index[None, :] >= ends[:, None]
    first_row = jnp.max(jnp.where(passed, ends[:, None], 0), axis=0)
    position = row_index - first_row
    frequency = 10000.0 ** (-2.0 * jnp.arange(HALF, dtype=F32) / HEAD_SIZE)
    angles = frequency[:, None] * position.astype(F32)[None, :]
    cosine, sine = jnp.cos(angles), jnp.sin(angles)
    low = first_row[::BLOCK] // BLOCK
    start = first_row[None, :]

    names = rank * expert_local + jnp.arange(expert_local, dtype=jnp.int32)
    member_all = jnp.any(
        routes[:, :, None] == jnp.arange(EXPERTS, dtype=jnp.int32)[None, None, :], axis=1
    )
    member = jnp.any(routes.T[None, :, :] == names[:, None, None], axis=1)
    count = jnp.sum(member.astype(jnp.int32), axis=1)
    table = jnp.sort(jnp.where(member, row_index[None, :], rows), axis=1)[:, :CAP]
    filled = jnp.arange(CAP, dtype=jnp.int32)[None, :] < count[:, None]
    is_high = (
        table[:, :, None] // 128 == jnp.arange(rows // 128, dtype=jnp.int32)[None, None, :]
    ).astype(BF16)
    is_low = table[:, :, None] % 128 == jnp.arange(128, dtype=jnp.int32)[None, None, :]

    normed_all, inverse_all = rms_norm(inputs_all.astype(F32), gain_one)
    hidden_one = normed_all.astype(BF16)
    qkv = dot(qkv_weight, hidden_one, 0, 1)
    q_t = (rope_t(qkv[:d_q], cosine, sine).astype(BF16).astype(F32) * HEAD_SIZE ** (-0.5)).astype(
        BF16
    )
    k_t = rope_t(qkv[d_q : d_q + d_k], cosine, sine).astype(BF16)
    v_t = qkv[d_q + d_k :].astype(BF16)
    k = jnp.transpose(k_t.reshape(kv_heads, HEAD_SIZE, rows), (0, 2, 1))
    v = jnp.transpose(v_t.reshape(kv_heads, HEAD_SIZE, rows), (0, 2, 1))
    o_t, lse, swapped = phase(
        lambda q_t, sent: list(attend(q_t, k, v_t, start, low)) + [swap_rows(sent)],
        [q_t, cotangent], [],
    )
    grad_all = join_rows(cotangent, swapped)
    inputs_f = tokens.astype(F32)
    residual_two = inputs_f + scatter_rows(dot(o_t, out_weight_t, 0, 1).astype(BF16))

    normed_two, inverse_two = rms_norm(residual_two, gain_two)
    hidden_rows = normed_two.astype(BF16)
    hidden_two = gather_rows(hidden_rows)
    logits = jnp.where(member_all, dot(hidden_two, router_weight, 1, 0), NEG)
    gates_f = jax.nn.softmax(logits, axis=-1)
    share = lax.dynamic_slice_in_dim(gates_f, rank * expert_local, expert_local, 1)
    picked = jnp.einsum(
        "esh,ehl->esl", is_high, share.astype(BF16).T.reshape(expert_local, rows // 128, 128),
        preferred_element_type=F32,
    )
    slot_gate = jnp.sum(jnp.where(is_low, picked, 0.0), axis=2, keepdims=True)

    calls = min(EXPERT_CALLS, expert_local)
    each = expert_local // calls
    parity = (me % 2).astype(jnp.int32).reshape(1)
    slots = table * (width // 128)
    out_part, dx_part = 0.0, 0.0
    dg, sums = [], []
    for call in range(calls):
        picked = slice(call * each, (call + 1) * each)
        made = []

        def work(counted, picked=picked, call=call, made=made):
            *outs, mark = expert_call(
                slots[picked].reshape(-1), counted, parity, hidden_two, grad_all, slot_gate,
                big, call * each, each,
            )
            made.extend(outs)
            return [mark]

        phase(work, [count[picked]], sums)
        keep, send, out_p, dx_p, dg_p = made
        sums.append(Reduce(keep, send))
        out_part = out_part + out_p.astype(F32)
        dx_part = dx_part + dx_p.astype(F32)
        dg.append(dg_p[:, :, 0])

    two_a, two_b = sums[2].split(3, 1)

    dg = jnp.where(filled, jnp.concatenate(dg, axis=0), 0.0)

    def over_x(sent, sent_out, dg):
        dg = jnp.where(is_low, dg[:, :, None], 0.0).astype(BF16)
        dg = jnp.einsum("esh,esl->ehl", is_high, dg, preferred_element_type=F32)
        dg = dg.reshape(expert_local, rows)
        d_dense = lax.dynamic_update_slice_in_dim(
            jnp.zeros((rows, EXPERTS), F32), dg.T, rank * expert_local, 1
        )
        return [scatter_rows(sent), scatter_rows(d_dense), sent_out]

    d_rows, d_gates, out_part = phase(
        over_x, [dx_part.astype(BF16), out_part.astype(BF16), dg],
        [sums[1], two_a, sums[3]],
    )
    three_a, three_b = sums[3].split(2, 2)
    gates_own = lax.dynamic_slice_in_dim(gates_f, own_row, local_rows, 0)
    d_logits = gates_own * (d_gates - jnp.sum(d_gates * gates_own, axis=-1, keepdims=True))
    router_grad = jnp.dot(hidden_rows.astype(F32).T, d_logits, precision=exact_mode)
    d_rows = d_rows + jnp.dot(d_logits, router_weight.astype(F32).T, precision=exact_mode)
    d_norm_two, gain_two_grad = rms_back(d_rows, residual_two, inverse_two, gain_two)
    d_residual = cotangent.astype(F32) + d_norm_two
    (d_all,) = phase(
        lambda sent: [gather_rows(sent)], [d_residual.astype(BF16)], [two_a, two_b, three_a]
    )

    do_t = dot(out_weight_t, d_all, 0, 1).astype(BF16)

    def back(do_t, out_part):
        parts = attend_back(
            0, kv_heads, q_t, do_t, o_t, lse, k, v, k_t, start, cosine, sine, low
        )
        return list(parts) + [scatter_rows(out_part)]

    dq_t, dk_t, dv_t, moe_rows = phase(
        back, [do_t, out_part], [two_b, three_a, three_b]
    )
    output = (residual_two + moe_rows).astype(BF16)
    d_qkv_t = jnp.concatenate([dq_t, dk_t, dv_t], axis=0)
    grad_out_t = dot(d_all, o_t, 0, 1).astype(BF16)
    grad_qkv = dot(hidden_one, d_qkv_t, 0, 1).astype(BF16)
    d_hidden_part = dot(d_qkv_t, qkv_weight, 0, 1)
    gain_one_grad = jnp.sum(d_hidden_part * inputs_all.astype(F32) * inverse_all, axis=0)
    misc = jnp.concatenate(
        [router_grad, gain_one_grad[:, None], gain_two_grad[:, None]], axis=1
    ).astype(BF16)
    misc = jnp.pad(misc, ((0, 0), (0, -misc.shape[1] % 128)))
    small_grad = jnp.concatenate([grad_qkv, grad_out_t, misc], axis=1)
    small_grad = small_grad.reshape(dp // 2, 2, shard_rows, small_grad.shape[1])
    even = parity[0] == 0
    first, second = small_grad[:, 0], small_grad[:, 1]
    small = Reduce(jnp.where(even, first, second), jnp.where(even, second, first))

    def end(sent):
        for _ in range(3):
            small.take(small.move(small.sends()))
        return [scatter_rows(sent), small.result()]

    d_hidden_one, small_sum = phase(end, [d_hidden_part.astype(BF16)], [three_b])
    d_norm_one, _ = rms_back(
        d_hidden_one, inputs_f, lax.dynamic_slice_in_dim(inverse_all, own_row, local_rows, 0),
        gain_one,
    )
    grad_tokens = (d_residual + d_norm_one).astype(BF16)

    ends = [sums[0], sums[1], two_a, two_b, three_a, three_b]
    total = jnp.concatenate([r.result() for r in ends if r is not None], axis=0)
    grad_gate, grad_up = total[:, 0], total[:, 1]
    half = shard_rows // 2
    grad_down = jnp.concatenate([total[:, 2, :half], total[:, 2, half:]], axis=2)
    over_tensor = small_sum[:, d_qkv + d_o : used]
    if tensor == 2:
        over_tensor = over_tensor + lax.ppermute(over_tensor, "tensor", [(0, 1), (1, 0)])
    else:
        over_tensor = lax.psum(over_tensor, "tensor")
    return (
        output,
        grad_tokens,
        over_tensor[:, EXPERTS],
        small_sum[:, :d_q],
        small_sum[:, d_q : d_q + d_k],
        small_sum[:, d_q + d_k : d_qkv],
        small_sum[:, d_qkv : d_qkv + d_o].T,
        over_tensor[:, EXPERTS + 1],
        over_tensor[:, :EXPERTS],
        grad_gate,
        grad_up,
        grad_down,
    )


def solution(mesh):
    return jax.shard_map(
        shards,
        mesh=mesh,
        in_specs=(
            P(("dp", "tensor"), None),
            P("dp", None),
            P("dp", None),
            P("dp"),
            P("dp", "tensor"),
            P("dp", "tensor"),
            P("dp", "tensor"),
            P("tensor", "dp"),
            P("dp"),
            P("dp", None),
            P("tensor", "dp", None),
            P("tensor", "dp", None),
            P("tensor", "dp", None),
            P(("dp", "tensor"), None),
        ),
        out_specs=(
            P(("dp", "tensor"), None),
            P(("dp", "tensor"), None),
            P("dp"),
            P("dp", "tensor"),
            P("dp", "tensor"),
            P("dp", "tensor"),
            P("tensor", "dp"),
            P("dp"),
            P("dp", None),
            P("tensor", "dp", None),
            P("tensor", "dp", None),
            P("tensor", "dp", None),
        ),
        check_vma=False,
    )
```

```python
import functools

import jax
import jax.numpy as jnp
from jax import lax
from jax.experimental import pallas as pl
from jax.experimental.pallas import tpu as pltpu
from jax.sharding import PartitionSpec as P

QUERY_HEADS = 16
KEY_VALUE_HEADS = 8
HEAD_SIZE = 64
HALF = HEAD_SIZE // 2
EXPERTS = 32
CAP = 768
TILE = 256
BLOCK = 256
STEP = 16
EXPERT_CALLS = 4
KERNEL_COST = pl.CostEstimate(flops=1, bytes_accessed=150 * 10**6, transcendentals=0)

exact_mode = lax.Precision.HIGHEST
F32 = jnp.float32
BF16 = jnp.bfloat16
NEG = -1e30


def dot(a, b, ca, cb):
    return lax.dot_general(a, b, (((ca,), (cb,)), ((), ())), preferred_element_type=F32)


def z_core_shape(dp):
    return (4, 2, 2) if dp == 16 else None


def gather_rows(x, axis="tensor"):
    n = lax.axis_size(axis)
    if n != 2:
        return lax.all_gather(x, axis, axis=0, tiled=True)
    rank = lax.axis_index(axis)
    other = lax.ppermute(x, axis, [(0, 1), (1, 0)])
    first = rank == 0
    return jnp.concatenate([jnp.where(first, x, other), jnp.where(first, other, x)], axis=0)


def swap_rows(x):
    if lax.axis_size("tensor") != 2:
        return lax.all_gather(x, "tensor", axis=0, tiled=True)
    return lax.ppermute(x, "tensor", [(0, 1), (1, 0)])


def join_rows(x, swapped):
    if lax.axis_size("tensor") != 2:
        return swapped
    first = lax.axis_index("tensor") == 0
    return jnp.concatenate([jnp.where(first, x, swapped), jnp.where(first, swapped, x)], axis=0)


def leave_rows(x):
    n = lax.axis_size("tensor")
    rows = x.shape[0] // n
    if n != 2:
        return None, x
    rank = lax.axis_index("tensor")
    return (
        lax.dynamic_slice_in_dim(x, rank * rows, rows, 0),
        lax.dynamic_slice_in_dim(x, (1 - rank) * rows, rows, 0),
    )


def swap_sums(x):
    if lax.axis_size("tensor") != 2:
        return lax.psum_scatter(x, "tensor", scatter_dimension=0, tiled=True)
    return lax.ppermute(x, "tensor", [(0, 1), (1, 0)])


def add_rows_of(own, swapped):
    return swapped.astype(F32) if own is None else own.astype(F32) + swapped.astype(F32)


def scatter_rows(x, axis="tensor"):
    n = lax.axis_size(axis)
    rows = x.shape[0] // n
    if n != 2:
        return lax.psum_scatter(x, axis, scatter_dimension=0, tiled=True).astype(F32)
    rank = lax.axis_index(axis)
    sent = lax.ppermute(
        lax.dynamic_slice_in_dim(x, (1 - rank) * rows, rows, 0), axis, [(0, 1), (1, 0)]
    )
    own = lax.dynamic_slice_in_dim(x, rank * rows, rows, 0)
    return own.astype(F32) + sent.astype(F32)


def dp_pairs(move):
    pairs = []
    for z in range(4):
        for y in range(2):
            for c in range(2):
                tz, ty, tc = move(z, y, c)
                pairs.append((z * 4 + y * 2 + c, tz * 4 + ty * 2 + tc))
    return pairs


CORE_PAIRS = dp_pairs(lambda z, y, c: (z, y, 1 - c))
Y_PAIRS = dp_pairs(lambda z, y, c: (z, 1 - y, c))
Z_PAIRS = {k: dp_pairs(lambda z, y, c, k=k: ((z + k) % 4, y, c)) for k in (1, 2, 3)}


def place(own, index, parts):
    buf = jnp.zeros((len(parts) + 1,) + own.shape, own.dtype)
    for i, a in [(index, own)] + parts:
        buf = lax.dynamic_update_index_in_dim(buf, a, i, 0)
    return buf


def gather_dp(x):
    n = lax.axis_size("dp")
    if z_core_shape(n) is None:
        return lax.all_gather(x, "dp", axis=0, tiled=False)
    me = lax.axis_index("dp")
    z, y, c = me // 4, (me // 2) % 2, me % 2
    parts = [((z - k) % 4, lax.ppermute(x, "dp", Z_PAIRS[k])) for k in (1, 3, 2)]
    buf = place(x, z, parts)
    buf = place(buf, y, [(1 - y, lax.ppermute(buf, "dp", Y_PAIRS))])
    buf = place(buf, c, [(1 - c, lax.ppermute(buf, "dp", CORE_PAIRS))])
    return jnp.transpose(buf, (2, 1, 0) + tuple(range(3, buf.ndim))).reshape((n,) + x.shape)


def at(a, i, axis):
    return lax.dynamic_index_in_dim(a, i, axis, keepdims=False)


def line_place():
    me = lax.axis_index("dp")
    return me // 4, (me // 2) % 2


class Reduce:
    def __init__(self, keep, send):
        self.by_hand = z_core_shape(lax.axis_size("dp")) is not None
        self.keep, self.send = keep, send
        self.stage = 0

    def split(self, *sizes):
        if not self.by_hand or sum(sizes) != self.keep.shape[1]:
            return [self] + [None] * (len(sizes) - 1)
        parts = []
        for i, size in enumerate(sizes):
            run = slice(sum(sizes[:i]), sum(sizes[:i]) + size)
            part = Reduce(self.keep[:, run], None)
            part.core, part.stage = self.core[:, run], 1
            parts.append(part)
        return parts

    def sends(self):
        if not self.by_hand:
            return []
        if self.stage == 0:
            return [self.send]
        z, y = line_place()
        if self.stage == 1:
            self.keep = self.keep.reshape((4, 2) + self.keep.shape[1:])
            self.core = self.core.reshape(self.keep.shape)
            return [
                (
                    at(self.keep, 1 - y, 1).astype(F32) + at(self.core, 1 - y, 1).astype(F32)
                ).astype(BF16)
            ]

        def line(i):
            return (
                at(at(self.keep, y, 1), i, 0).astype(F32)
                + at(at(self.core, y, 1), i, 0).astype(F32)
                + at(self.over, i, 0).astype(F32)
            )

        self.own = line(z)
        return [line((z + k) % 4).astype(BF16) for k in (2, 1, 3)]

    def move(self, sent):
        if not self.by_hand:
            return []
        pairs = ([CORE_PAIRS], [Y_PAIRS], [Z_PAIRS[k] for k in (2, 1, 3)])[self.stage]
        return [lax.ppermute(a, "dp", p) for a, p in zip(sent, pairs)]

    def take(self, got):
        if self.by_hand:
            if self.stage == 0:
                (self.core,) = got
            elif self.stage == 1:
                (self.over,) = got
            else:
                self.parts = got
        self.stage += 1

    def result(self):
        n = lax.axis_size("dp")
        if not self.by_hand:
            even = lax.axis_index("dp") % 2 == 0
            first = jnp.where(even, self.keep, self.send)
            second = jnp.where(even, self.send, self.keep)
            both = jnp.stack([first, second], axis=1).reshape((n,) + self.keep.shape[1:])
            return lax.psum_scatter(both, "dp", scatter_dimension=0, tiled=False).astype(F32)
        total = self.own
        for a in self.parts:
            total = total + a.astype(F32)
        return total


class Joined:
    def __init__(self, *reduces):
        self.reduces = [r for r in reduces if r is not None]

    def sends(self):
        self.axis = (1, 1, 0)[self.reduces[0].stage]
        self.sizes, lists = [], [r.sends() for r in self.reduces]
        if not lists[0]:
            return []
        self.sizes = [a[0].shape[self.axis] for a in lists]
        return [jnp.concatenate(parts, axis=self.axis) for parts in zip(*lists)]

    def move(self, sent):
        return self.reduces[0].move(sent)

    def take(self, got):
        begin = 0
        for r, size in zip(self.reduces, self.sizes or [0] * len(self.reduces)):
            r.take([lax.slice_in_dim(a, begin, begin + size, axis=self.axis) for a in got])
            begin += size


def phase(work, inputs, reduces):
    sends = [r.sends() for r in reduces]
    (inputs, sends) = lax.optimization_barrier((list(inputs), sends))
    results = work(*inputs)
    moved = [r.move(sent) for r, sent in zip(reduces, sends)]
    results, moved = lax.optimization_barrier((results, moved))
    for r, got in zip(reduces, moved):
        r.take(got)
    return results


def rms_norm(values, gain):
    inverse = lax.rsqrt(jnp.mean(values * values, axis=-1, keepdims=True) + 1e-06)
    return (values * inverse * gain, inverse)


def rms_back(grad_rows, values, inverse, gain):
    scaled = grad_rows * gain
    gain_grad = jnp.sum(grad_rows * values * inverse, axis=0)
    inner = jnp.mean(scaled * values, axis=-1, keepdims=True)
    return (inverse * scaled - values * inverse * inverse * inverse * inner, gain_grad)


def rope_t(values, cosine, sine):
    rows = values.shape[1]
    v = values.reshape(-1, 2, HALF, rows)
    one, two = v[:, 0], v[:, 1]
    return jnp.stack(
        [one * cosine - two * sine, two * cosine + one * sine], axis=1
    ).reshape(values.shape)


def mask_of(start, j, i, bq):
    key = j * BLOCK + lax.broadcasted_iota(jnp.int32, (BLOCK, 2 * bq), 0)
    query = lax.broadcasted_iota(jnp.int32, (BLOCK, 2 * bq), 1)
    query = i * bq + jnp.where(query >= bq, query - bq, query)
    return (key >= start) & (key <= query)


def attend_kernel(low, q_ref, k_ref, v_ref, start_ref, o_ref, lse_ref):
    i = pl.program_id(1)
    bq = BLOCK
    q = q_ref[...]
    qs = jnp.concatenate([q[:HEAD_SIZE], q[HEAD_SIZE:]], axis=1)
    start = start_ref[...]
    start = jnp.concatenate([start, start], axis=1)

    def step(j, carry):
        peak, total, acc = carry
        at_key = pl.ds(pl.multiple_of(j * BLOCK, BLOCK), BLOCK)
        s = dot(k_ref[0, at_key, :], qs, 1, 0)
        s = jnp.where(mask_of(start, j, i, bq), s, NEG)
        new = jnp.maximum(peak, jnp.max(s, axis=0, keepdims=True))
        p = jnp.exp(s - new)
        scale = jnp.exp(peak - new)
        total = total * scale + jnp.sum(p, axis=0, keepdims=True)
        acc = acc * scale + dot(v_ref[:, at_key], p.astype(BF16), 1, 0)
        return new, total, acc

    peak, total, acc = lax.fori_loop(
        low[i],
        i + 1,
        step,
        (
            jnp.full((1, 2 * bq), NEG, F32),
            jnp.zeros((1, 2 * bq), F32),
            jnp.zeros((HEAD_SIZE, 2 * bq), F32),
        ),
    )
    out = (acc / total).astype(BF16)
    o_ref[...] = jnp.concatenate([out[:, :bq], out[:, bq:]], axis=0)
    lse = peak + jnp.log(total)
    lse_ref[0] = jnp.concatenate([lse[:, :bq], lse[:, bq:]], axis=0)


def attend(q_t, k, v_t, start, low):
    rows = q_t.shape[1]
    heads = k.shape[0]
    blocks = rows // BLOCK
    return pl.pallas_call(
        attend_kernel,
        grid_spec=pltpu.PrefetchScalarGridSpec(
            num_scalar_prefetch=1,
            grid=(heads, blocks),
            in_specs=[
                pl.BlockSpec((2 * HEAD_SIZE, BLOCK), lambda h, i, low: (h, i)),
                pl.BlockSpec((1, rows, HEAD_SIZE), lambda h, i, low: (h, 0, 0)),
                pl.BlockSpec((HEAD_SIZE, rows), lambda h, i, low: (h, 0)),
                pl.BlockSpec((1, BLOCK), lambda h, i, low: (0, i)),
            ],
            out_specs=[
                pl.BlockSpec((2 * HEAD_SIZE, BLOCK), lambda h, i, low: (h, i)),
                pl.BlockSpec((1, 2, BLOCK), lambda h, i, low: (h, 0, i)),
            ],
        ),
        out_shape=[
            jax.ShapeDtypeStruct(q_t.shape, BF16),
            jax.ShapeDtypeStruct((heads, 2, rows), F32),
        ],
        cost_estimate=KERNEL_COST,
        name="attend",
    )(low, q_t, k, v_t, start)


def attend_back_kernel(
    low, q_ref, do_ref, o_ref, lse_ref, k_ref, v_ref, kt_ref, start_ref, cos_ref, sin_ref,
    dq_ref, dk_ref, dv_ref, dk_sum, dv_sum,
):
    i = pl.program_id(1)
    bq = BLOCK

    @pl.when(i == 0)
    def _():
        dk_sum[...] = jnp.zeros_like(dk_sum)
        dv_sum[...] = jnp.zeros_like(dv_sum)

    def side(a):
        return jnp.concatenate([a[:HEAD_SIZE], a[HEAD_SIZE:]], axis=1)

    qs = side(q_ref[...])
    dos = side(do_ref[...])
    inner = jnp.sum(dos.astype(F32) * side(o_ref[...]).astype(F32), axis=0, keepdims=True)
    lse = lse_ref[0]
    lse = jnp.concatenate([lse[0:1], lse[1:2]], axis=1)
    start = start_ref[...]
    start = jnp.concatenate([start, start], axis=1)

    def step(j, dq):
        at_key = pl.ds(pl.multiple_of(j * BLOCK, BLOCK), BLOCK)
        s = dot(k_ref[0, at_key, :], qs, 1, 0)
        p = jnp.where(mask_of(start, j, i, bq), jnp.exp(s - lse), 0.0)
        dp = dot(v_ref[0, at_key, :], dos, 1, 0)
        ds = (p * (dp - inner)).astype(BF16)
        dv_sum[at_key, :] += dot(p.astype(BF16), dos, 1, 1)
        dk_sum[at_key, :] += dot(ds, qs, 1, 1)
        return dq + dot(kt_ref[:, at_key], ds, 1, 0)

    dq = lax.fori_loop(low[i], i + 1, step, jnp.zeros((HEAD_SIZE, 2 * bq), F32))
    dq = dq * HEAD_SIZE ** (-0.5)
    here = pl.ds(pl.multiple_of(i * bq, bq), bq)

    def turn_back(v, cosine, sine):
        one, two = v[:HALF], v[HALF:]
        return jnp.concatenate(
            [one * cosine + two * sine, two * cosine - one * sine], axis=0
        ).astype(BF16)

    for h in range(2):
        dq_ref[h * HEAD_SIZE : (h + 1) * HEAD_SIZE, :] = turn_back(
            dq[:, h * bq : (h + 1) * bq], cos_ref[:, here], sin_ref[:, here]
        )

    @pl.when(i == pl.num_programs(1) - 1)
    def _():
        dk_ref[...] = turn_back(dk_sum[...].T, cos_ref[...], sin_ref[...])
        dv_ref[...] = dv_sum[...].T.astype(BF16)


def attend_back(first, heads, q_t, do_t, o_t, lse, k, v, k_t, start, cosine, sine, low):
    rows = q_t.shape[1]
    blocks = rows // BLOCK
    pair = pl.BlockSpec((2 * HEAD_SIZE, BLOCK), lambda h, i, low: (h + first, i))
    whole = pl.BlockSpec((1, rows, HEAD_SIZE), lambda h, i, low: (h + first, 0, 0))
    table = pl.BlockSpec((HALF, rows), lambda h, i, low: (0, 0))
    grad = pl.BlockSpec((HEAD_SIZE, rows), lambda h, i, low: (h, 0))
    return pl.pallas_call(
        attend_back_kernel,
        grid_spec=pltpu.PrefetchScalarGridSpec(
            num_scalar_prefetch=1,
            grid=(heads, blocks),
            in_specs=[
                pair,
                pair,
                pair,
                pl.BlockSpec((1, 2, BLOCK), lambda h, i, low: (h + first, 0, i)),
                whole,
                whole,
                pl.BlockSpec((HEAD_SIZE, rows), lambda h, i, low: (h + first, 0)),
                pl.BlockSpec((1, BLOCK), lambda h, i, low: (0, i)),
                table,
                table,
            ],
            out_specs=[
                pl.BlockSpec((2 * HEAD_SIZE, BLOCK), lambda h, i, low: (h, i)), grad, grad,
            ],
            scratch_shapes=[
                pltpu.VMEM((rows, HEAD_SIZE), F32), pltpu.VMEM((rows, HEAD_SIZE), F32),
            ],
        ),
        out_shape=[
            jax.ShapeDtypeStruct((heads * 2 * HEAD_SIZE, rows), BF16),
            jax.ShapeDtypeStruct((heads * HEAD_SIZE, rows), BF16),
            jax.ShapeDtypeStruct((heads * HEAD_SIZE, rows), BF16),
        ],
        cost_estimate=KERNEL_COST,
        name="attend_back",
    )(low, q_t, do_t, o_t, lse, k, v, k_t, start, cosine, sine)


def pieces_of(rows, most):
    return [(r, min(most, rows - r)) for r in range(0, rows, most)]


def expert_kernel(
    table, count, parity, x_hbm, c_hbm, gate_ref, w_ref, keep_ref, send_ref, out_hbm, dx_hbm,
    dg_ref, mark_ref, xs, cs, oacc, dacc, xg, cg, xb, cb, dab, hgb, sems,
):
    e = pl.program_id(0)
    last = pl.num_programs(0) - 1
    rows, width = x_hbm.shape
    lanes = width // 128
    dp, rs, ff = w_ref.shape[0], w_ref.shape[3], w_ref.shape[4]
    stages = (xb, cb, dab)

    @pl.when(e == 0)
    def _():
        jobs = [
            (source.at[pl.ds(r, n), :], target, r, n)
            for source, target in ((x_hbm, xs), (c_hbm, cs))
            for r, n in pieces_of(rows, CAP)
        ]
        copies = [
            pltpu.make_async_copy(
                source, stages[i % 3].at[pl.ds(0, n), :], sems.at[i % 3]
            )
            for i, (source, _, _, n) in enumerate(jobs)
        ]
        for op in copies[:3]:
            op.start()
        oacc[...] = jnp.zeros_like(oacc)
        dacc[...] = jnp.zeros_like(dacc)
        xg[...] = jnp.zeros_like(xg)
        cg[...] = jnp.zeros_like(cg)
        for i, (_, target, r, n) in enumerate(jobs):
            copies[i].wait()
            for j in range(lanes):
                target[pl.ds(r * lanes + j, n, stride=lanes), :] = stages[i % 3][
                    :n, j * 128 : (j + 1) * 128
                ].astype(F32)
            if i + 3 < len(jobs):
                copies[i + 3].start()
        for target in (xs, cs):
            target[rows * lanes :, :] = jnp.zeros((8 * lanes, 128), F32)

    named = count[e]
    w_gate = w_ref[:, 0, 0].reshape(dp * rs, ff)
    w_up = w_ref[:, 0, 1].reshape(dp * rs, ff)
    w_low = w_ref[:, 0, 2, : rs // 2].reshape(dp * rs // 2, ff)
    w_high = w_ref[:, 0, 2, rs // 2 :].reshape(dp * rs // 2, ff)

    for t in range(CAP // TILE):
        here = slice(t * TILE, (t + 1) * TILE)

        @pl.when(named > t * TILE)
        def _(t=t, here=here):
            groups = (jnp.minimum(named - t * TILE, TILE) + STEP - 1) // STEP
            first = e * CAP + t * TILE

            def places(b):
                return [
                    pl.ds(pl.multiple_of(table[first + b * STEP + k], 8), lanes)
                    for k in range(STEP)
                ]

            def own(b):
                return [
                    pl.ds(pl.multiple_of(b * (STEP * lanes) + k * lanes, 8), lanes)
                    for k in range(STEP)
                ]

            def pick(b, carry):
                there, here_ = places(b), own(b)
                xrows = [xs[p, :] for p in there]
                crows = [cs[p, :] for p in there]
                for p, v, w in zip(here_, xrows, crows):
                    xg[p, :] = v
                    cg[p, :] = w
                return carry

            lax.fori_loop(0, groups, pick, 0)
            for j in range(lanes):
                one = slice(j * 128, (j + 1) * 128)
                xb[here, one] = xg[pl.ds(j, TILE, stride=lanes), :].astype(BF16)
                cb[here, one] = cg[pl.ds(j, TILE, stride=lanes), :].astype(BF16)
            gate = gate_ref[0, here, :]
            x = xb[here, :]
            c = cb[here, :]
            a = dot(x, w_gate, 1, 0)
            b = dot(x, w_up, 1, 0)
            sig = jax.nn.sigmoid(a)
            silu = a * sig
            hid = silu * b
            hg = (hid * gate).astype(BF16)
            hgb[here, :] = hg
            u = dot(c[:, :ff], w_low, 1, 1) + dot(c[:, ff:], w_high, 1, 1)
            dg_ref[0, here, :] = jnp.sum(hid * u, axis=1, keepdims=True)
            du = gate * u
            da = (du * b * sig * (1.0 + a * (1.0 - sig))).astype(BF16)
            db = (du * silu).astype(BF16)
            dab[here, :ff] = da
            dab[here, ff:] = db
            for half, w in enumerate((w_low, w_high)):
                y = dot(hg, w, 1, 0)
                for j in range(ff // 128):
                    xg[pl.ds(half * (ff // 128) + j, TILE, stride=lanes), :] = y[
                        :, j * 128 : (j + 1) * 128
                    ]
            dx = dot(da, w_gate, 1, 1) + dot(db, w_up, 1, 1)
            for j in range(lanes):
                cg[pl.ds(j, TILE, stride=lanes), :] = dx[:, j * 128 : (j + 1) * 128]

            def add(b, carry):
                there, here_ = places(b), own(b)
                outs = [oacc[p, :] + xg[q, :] for p, q in zip(there, here_)]
                backs = [dacc[p, :] + cg[q, :] for p, q in zip(there, here_)]
                for p, v, w in zip(there, outs, backs):
                    oacc[p, :] = v
                    dacc[p, :] = w
                return carry

            lax.fori_loop(0, groups, add, 0)

    even = parity[0] == 0

    def split(value, slot, low, high):
        v = value.reshape(dp // 2, 2, high - low, ff)
        first, second = v[:, 0], v[:, 1]
        keep_ref[:, 0, slot, low:high, :] = jnp.where(even, first, second)
        send_ref[:, 0, slot, low:high, :] = jnp.where(even, second, first)

    def grads(depth):
        x = xb[:depth, :]
        d = dab[:depth, :]
        split(dot(x, d[:, :ff], 0, 0).astype(BF16), 0, 0, rs)
        split(dot(x, d[:, ff:], 0, 0).astype(BF16), 1, 0, rs)
        h = hgb[:depth, :]
        c = cb[:depth, :]
        split(dot(h, c[:, :ff], 0, 0).astype(BF16), 2, 0, rs // 2)
        split(dot(h, c[:, ff:], 0, 0).astype(BF16), 2, rs // 2, rs)

    @pl.when(named == 0)
    def _():
        keep_ref[...] = jnp.zeros_like(keep_ref)
        send_ref[...] = jnp.zeros_like(send_ref)

    for t in range(CAP // TILE):

        @pl.when((named > t * TILE) & (named <= (t + 1) * TILE))
        def _(t=t):
            grads((t + 1) * TILE)

    @pl.when(e == last)
    def _():
        mark_ref[...] = jnp.zeros_like(mark_ref)
        jobs = [
            (source, target.at[pl.ds(r, n), :], r, n)
            for source, target in ((oacc, out_hbm), (dacc, dx_hbm))
            for r, n in pieces_of(rows, CAP)
        ]
        copies = [
            pltpu.make_async_copy(
                stages[i % 3].at[pl.ds(0, n), :], target, sems.at[i % 3]
            )
            for i, (_, target, _, n) in enumerate(jobs)
        ]
        for i, (source, _, r, n) in enumerate(jobs):
            if i >= 3:
                copies[i - 3].wait()
            for j in range(lanes):
                stages[i % 3][:n, j * 128 : (j + 1) * 128] = source[
                    pl.ds(r * lanes + j, n, stride=lanes), :
                ].astype(BF16)
            copies[i].start()
        for op in copies[-3:]:
            op.wait()


def expert_call(table, count, parity, x, c, gates, weights, first_expert, expert_count):
    rows, width = x.shape
    dp, _, _, rs, ff = weights.shape
    lanes = width // 128
    grads = pl.BlockSpec((dp // 2, 1, 3, rs, ff), lambda e, *_: (0, e, 0, 0, 0))
    hbm = pl.BlockSpec(memory_space=pl.ANY)
    return pl.pallas_call(
        expert_kernel,
        grid_spec=pltpu.PrefetchScalarGridSpec(
            num_scalar_prefetch=3,
            grid=(expert_count,),
            in_specs=[
                hbm,
                hbm,
                pl.BlockSpec((1, CAP, 1), lambda e, *_: (e + first_expert, 0, 0)),
                pl.BlockSpec(
                    (dp, 1, 3, rs, ff), lambda e, *_: (0, e + first_expert, 0, 0, 0)
                ),
            ],
            out_specs=[
                grads, grads, hbm, hbm, pl.BlockSpec((1, CAP, 1), lambda e, *_: (e, 0, 0)),
                pl.BlockSpec((8, 128), lambda e, *_: (0, 0)),
            ],
            scratch_shapes=[
                pltpu.VMEM(((rows + 8) * lanes, 128), F32),
                pltpu.VMEM(((rows + 8) * lanes, 128), F32),
                pltpu.VMEM(((rows + 8) * lanes, 128), F32),
                pltpu.VMEM(((rows + 8) * lanes, 128), F32),
                pltpu.VMEM((TILE * lanes, 128), F32),
                pltpu.VMEM((TILE * lanes, 128), F32),
                pltpu.VMEM((CAP, width), BF16),
                pltpu.VMEM((CAP, width), BF16),
                pltpu.VMEM((CAP, 2 * ff), BF16),
                pltpu.VMEM((CAP, ff), BF16),
                pltpu.SemaphoreType.DMA((3,)),
            ],
        ),
        out_shape=[
            jax.ShapeDtypeStruct((dp // 2, expert_count, 3, rs, ff), BF16),
            jax.ShapeDtypeStruct((dp // 2, expert_count, 3, rs, ff), BF16),
            jax.ShapeDtypeStruct((rows, width), BF16),
            jax.ShapeDtypeStruct((rows, width), BF16),
            jax.ShapeDtypeStruct((expert_count, CAP, 1), F32),
            jax.ShapeDtypeStruct((8, 128), F32),
        ],
        compiler_params=pltpu.CompilerParams(vmem_limit_bytes=63 * 2**20),
        cost_estimate=KERNEL_COST,
        name="experts",
    )(table, count, parity, x, c, gates, weights)


def shards(
    tokens, lengths, routes, norm1_gain, w_query, key_projection, value_projection, w_out,
    norm2_gain, w_router, w_gate, w_up, w_down, cotangent,
):
    tensor = lax.axis_size("tensor")
    rank = lax.axis_index("tensor")
    dp = lax.axis_size("dp")
    me = lax.axis_index("dp")
    local_rows, width = tokens.shape
    rows = local_rows * tensor
    heads = QUERY_HEADS // tensor
    kv_heads = KEY_VALUE_HEADS // tensor
    expert_local = w_gate.shape[0]
    shard_rows = norm1_gain.shape[0]
    own_row = rank * local_rows

    pack = jnp.concatenate(
        [
            w_query, key_projection, value_projection, w_out.T, w_router,
            norm1_gain[:, None], norm2_gain[:, None],
        ],
        axis=1,
    )
    used = pack.shape[1]
    pack = jnp.pad(pack, ((0, 0), (0, -used % 128)))
    small = gather_dp(pack).reshape(dp * shard_rows, pack.shape[1])
    d_qkv = w_query.shape[1] + 2 * key_projection.shape[1]
    d_q, d_k = w_query.shape[1], key_projection.shape[1]
    d_o = w_out.shape[0]
    qkv_weight = small[:, :d_qkv]
    out_weight_t = small[:, d_qkv : d_qkv + d_o]
    router_weight = small[:, d_qkv + d_o : d_qkv + d_o + EXPERTS]
    gains = small[:, used - 2 : used].astype(F32).T
    gain_one, gain_two = gains[0], gains[1]

    ff = w_gate.shape[2]
    down = jnp.concatenate([w_down[:, :, :ff], w_down[:, :, ff:]], axis=1)
    big_shard = jnp.stack([w_gate, w_up, down], axis=1)
    big = lax.all_gather(big_shard.reshape(-1, ff), "dp", axis=0, tiled=True)
    big = big.reshape((dp,) + big_shard.shape)

    inputs_all = gather_rows(tokens)

    seq = lengths[0]
    order = jnp.arange(seq.shape[0], dtype=jnp.int32)
    ends = jnp.sum(jnp.where(order[:, None] <= order[None, :], seq[:, None], 0), axis=0)
    row_index = jnp.arange(rows, dtype=jnp.int32)
    passed = row_index[None, :] >= ends[:, None]
    first_row = jnp.max(jnp.where(passed, ends[:, None], 0), axis=0)
    position = row_index - first_row
    frequency = 10000.0 ** (-2.0 * jnp.arange(HALF, dtype=F32) / HEAD_SIZE)
    angles = frequency[:, None] * position.astype(F32)[None, :]
    cosine, sine = jnp.cos(angles), jnp.sin(angles)
    low = first_row[::BLOCK] // BLOCK
    start = first_row[None, :]

    names = rank * expert_local + jnp.arange(expert_local, dtype=jnp.int32)
    member_all = jnp.any(
        routes[:, :, None] == jnp.arange(EXPERTS, dtype=jnp.int32)[None, None, :], axis=1
    )
    member = jnp.any(routes.T[None, :, :] == names[:, None, None], axis=1)
    count = jnp.sum(member.astype(jnp.int32), axis=1)
    table = jnp.sort(jnp.where(member, row_index[None, :], rows), axis=1)[:, :CAP]
    filled = jnp.arange(CAP, dtype=jnp.int32)[None, :] < count[:, None]
    is_high = (
        table[:, :, None] // 128 == jnp.arange(rows // 128, dtype=jnp.int32)[None, None, :]
    ).astype(BF16)
    is_low = table[:, :, None] % 128 == jnp.arange(128, dtype=jnp.int32)[None, None, :]

    normed_all, inverse_all = rms_norm(inputs_all.astype(F32), gain_one)
    hidden_one = normed_all.astype(BF16)
    qkv = dot(qkv_weight, hidden_one, 0, 1)
    q_t = (rope_t(qkv[:d_q], cosine, sine).astype(BF16).astype(F32) * HEAD_SIZE ** (-0.5)).astype(
        BF16
    )
    k_t = rope_t(qkv[d_q : d_q + d_k], cosine, sine).astype(BF16)
    v_t = qkv[d_q + d_k :].astype(BF16)
    k = jnp.transpose(k_t.reshape(kv_heads, HEAD_SIZE, rows), (0, 2, 1))
    v = jnp.transpose(v_t.reshape(kv_heads, HEAD_SIZE, rows), (0, 2, 1))
    o_t, lse, swapped = phase(
        lambda q_t, sent: list(attend(q_t, k, v_t, start, low)) + [swap_rows(sent)],
        [q_t, cotangent], [],
    )
    grad_all = join_rows(cotangent, swapped)
    inputs_f = tokens.astype(F32)
    residual_two = inputs_f + scatter_rows(dot(o_t, out_weight_t, 0, 1).astype(BF16))

    normed_two, inverse_two = rms_norm(residual_two, gain_two)
    hidden_rows = normed_two.astype(BF16)
    hidden_two = gather_rows(hidden_rows)
    logits = jnp.where(member_all, dot(hidden_two, router_weight, 1, 0), NEG)
    gates_f = jax.nn.softmax(logits, axis=-1)
    share = lax.dynamic_slice_in_dim(gates_f, rank * expert_local, expert_local, 1)
    picked = jnp.einsum(
        "esh,ehl->esl", is_high, share.astype(BF16).T.reshape(expert_local, rows // 128, 128),
        preferred_element_type=F32,
    )
    slot_gate = jnp.sum(jnp.where(is_low, picked, 0.0), axis=2, keepdims=True)

    calls = min(EXPERT_CALLS, expert_local)
    each = expert_local // calls
    parity = (me % 2).astype(jnp.int32).reshape(1)
    slots = table * (width // 128)
    parts, sums = [], []
    for call in range(calls):
        picked = slice(call * each, (call + 1) * each)

        def work(counted, picked=picked, call=call):
            return list(
                expert_call(
                    slots[picked].reshape(-1), counted, parity, hidden_two, grad_all, slot_gate,
                    big, call * each, each,
                )[:5]
            )

        keep, send, out_p, dx_p, dg_p = phase(work, [count[picked]], sums)
        sums.append(Reduce(keep, send))
        parts.append((out_p, dx_p, dg_p))

    two_a, two_b = sums[2].split(3, 1)

    def total_of(*flat):
        outs, backs, dgs = flat[:calls], flat[calls : 2 * calls], flat[2 * calls :]
        out_part = functools.reduce(jnp.add, [o.astype(F32) for o in outs]).astype(BF16)
        dx_part = functools.reduce(jnp.add, [o.astype(F32) for o in backs]).astype(BF16)
        dg = jnp.where(filled, jnp.concatenate([d[:, :, 0] for d in dgs], axis=0), 0.0)
        dg = jnp.where(is_low, dg[:, :, None], 0.0).astype(BF16)
        dg = jnp.einsum("esh,esl->ehl", is_high, dg, preferred_element_type=F32)
        dg = dg.reshape(expert_local, rows)
        d_dense = lax.dynamic_update_slice_in_dim(
            jnp.zeros((rows, 128), BF16), dg.T.astype(BF16), rank * expert_local, 1
        )
        own, sent = leave_rows(jnp.concatenate([dx_part, d_dense], axis=1))
        return [out_part, sent] + ([] if own is None else [own])

    out_part, sent, *own = phase(total_of, [a for p in zip(*parts) for a in p], [sums[3]])
    three_a, three_b = sums[3].split(2, 2)
    (swapped,) = phase(lambda sent: [swap_sums(sent)], [sent], [sums[1], two_a])
    d_both = add_rows_of(own[0] if own else None, swapped)
    d_rows, d_gates = d_both[:, :width], d_both[:, width : width + EXPERTS]
    gates_own = lax.dynamic_slice_in_dim(gates_f, own_row, local_rows, 0)
    d_logits = gates_own * (d_gates - jnp.sum(d_gates * gates_own, axis=-1, keepdims=True))
    router_grad = jnp.dot(hidden_rows.astype(F32).T, d_logits, precision=exact_mode)
    d_rows = d_rows + jnp.dot(d_logits, router_weight.astype(F32).T, precision=exact_mode)
    d_norm_two, gain_two_grad = rms_back(d_rows, residual_two, inverse_two, gain_two)
    d_residual = cotangent.astype(F32) + d_norm_two
    d_sent = d_residual.astype(BF16)
    (swapped,) = phase(
        lambda sent: [swap_rows(sent)], [d_sent], [two_a, Joined(two_b, three_a)]
    )
    d_all = join_rows(d_sent, swapped)

    do_t = dot(out_weight_t, d_all, 0, 1).astype(BF16)

    moe_own, moe_sent = leave_rows(out_part)

    def back(do_t, sent):
        parts = attend_back(
            0, kv_heads, q_t, do_t, o_t, lse, k, v, k_t, start, cosine, sine, low
        )
        return list(parts) + [swap_sums(sent)]

    dq_t, dk_t, dv_t, swapped = phase(
        back, [do_t, moe_sent], [Joined(two_b, three_a)] + [r for r in [three_b] if r is not None]
    )
    moe_rows = add_rows_of(moe_own, swapped)
    output = (residual_two + moe_rows).astype(BF16)
    d_qkv_t = jnp.concatenate([dq_t, dk_t, dv_t], axis=0)
    d_hidden_part = dot(d_qkv_t, qkv_weight, 0, 1)
    end_own, end_sent = leave_rows(d_hidden_part.astype(BF16))
    halves = 2 if tensor == 2 else 1
    size = end_sent.shape[0] // halves

    def grads(d_qkv_t, d_part, sent):
        grad_out_t = dot(d_all, o_t, 0, 1).astype(BF16)
        grad_qkv = dot(hidden_one, d_qkv_t, 0, 1).astype(BF16)
        gain_one_grad = jnp.sum(d_part * inputs_all.astype(F32) * inverse_all, axis=0)
        misc = jnp.concatenate(
            [router_grad, gain_one_grad[:, None], gain_two_grad[:, None]], axis=1
        ).astype(BF16)
        misc = jnp.pad(misc, ((0, 0), (0, -misc.shape[1] % 128)))
        small_grad = jnp.concatenate([grad_qkv, grad_out_t, misc], axis=1)
        small_grad = small_grad.reshape(dp // 2, 2, shard_rows, small_grad.shape[1])
        even = parity[0] == 0
        first, second = small_grad[:, 0], small_grad[:, 1]
        return [
            jnp.where(even, first, second), jnp.where(even, second, first), swap_sums(sent),
        ]

    keep, send, swapped = phase(
        grads, [d_qkv_t, d_hidden_part, end_sent[:size]],
        [r for r in [three_b] if r is not None],
    )
    small = Reduce(keep, send)

    def end(sent):
        for _ in range(3):
            small.take(small.move(small.sends()))
        return [small.result()] + ([swap_sums(sent)] if halves == 2 else [])

    small_sum, *rest = phase(end, [end_sent[size:]], [])
    d_hidden_one = add_rows_of(end_own, jnp.concatenate([swapped] + rest, axis=0))
    d_norm_one, _ = rms_back(
        d_hidden_one, inputs_f, lax.dynamic_slice_in_dim(inverse_all, own_row, local_rows, 0),
        gain_one,
    )
    grad_tokens = (d_residual + d_norm_one).astype(BF16)

    ends = [sums[0], sums[1], two_a, two_b, three_a, three_b]
    total = jnp.concatenate([r.result() for r in ends if r is not None], axis=0)
    grad_gate, grad_up = total[:, 0], total[:, 1]
    half = shard_rows // 2
    grad_down = jnp.concatenate([total[:, 2, :half], total[:, 2, half:]], axis=2)
    over_tensor = small_sum[:, d_qkv + d_o : used]
    if tensor == 2:
        over_tensor = over_tensor + lax.ppermute(over_tensor, "tensor", [(0, 1), (1, 0)])
    else:
        over_tensor = lax.psum(over_tensor, "tensor")
    return (
        output,
        grad_tokens,
        over_tensor[:, EXPERTS],
        small_sum[:, :d_q],
        small_sum[:, d_q : d_q + d_k],
        small_sum[:, d_q + d_k : d_qkv],
        small_sum[:, d_qkv : d_qkv + d_o].T,
        over_tensor[:, EXPERTS + 1],
        over_tensor[:, :EXPERTS],
        grad_gate,
        grad_up,
        grad_down,
    )


def solution(mesh):
    return jax.shard_map(
        shards,
        mesh=mesh,
        in_specs=(
            P(("dp", "tensor"), None),
            P("dp", None),
            P("dp", None),
            P("dp"),
            P("dp", "tensor"),
            P("dp", "tensor"),
            P("dp", "tensor"),
            P("tensor", "dp"),
            P("dp"),
            P("dp", None),
            P("tensor", "dp", None),
            P("tensor", "dp", None),
            P("tensor", "dp", None),
            P(("dp", "tensor"), None),
        ),
        out_specs=(
            P(("dp", "tensor"), None),
            P(("dp", "tensor"), None),
            P("dp"),
            P("dp", "tensor"),
            P("dp", "tensor"),
            P("dp", "tensor"),
            P("tensor", "dp"),
            P("dp"),
            P("dp", None),
            P("tensor", "dp", None),
            P("tensor", "dp", None),
            P("tensor", "dp", None),
        ),
        check_vma=False,
    )
```
